512 devices in a mesh: dp: 8 (over y), ctx: 64 (over z, x, core).
Axes of the slice: x: 4, y: 8, z: 8, core: 2. Of those that a mesh axis runs over, the one named last changes fastest.
Arguments:
- q_stream: bfloat16 [8192, 4096], P('ctx', 'dp'), may hold values from -6 to 6
- k_stream: bfloat16 [8192, 4096], P('ctx', 'dp'), may hold values from -6 to 6
- v_stream: bfloat16 [8192, 4096], P('ctx', 'dp'), may hold values from -6 to 6
- filter_taps: float32 [128, 4096], P('dp'), may hold values from -0.6 to 0.6
- short_taps: float32 [9, 4096], P(None, 'dp'), may hold values from -3 to 3
- cotangent: bfloat16 [8192, 4096], P('ctx', 'dp'), may hold values from -6 to 6
Outputs:
- mixed: bfloat16 [8192, 4096], P('ctx', 'dp')
- grad_q: bfloat16 [8192, 4096], P('ctx', 'dp')
- grad_k: bfloat16 [8192, 4096], P('ctx', 'dp')
- grad_v: bfloat16 [8192, 4096], P('ctx', 'dp')
- grad_filter: float32 [128, 4096], P('dp')
- grad_short: float32 [9, 4096], P(None, 'dp')
The draws below stay inside these ranges and needn't reach their ends.
All inputs are finite; a program needn't handle non-finite values.
Results may differ from the reference program's by a relative error of at most 0.00175.
Values may be sent and summed in bfloat16 or wider, within the bound.
No kernel may reach another device: no remote copies, remote signals or barrier semaphores. Data moves between devices by JAX's collectives and lax.ppermute only.
A program may use at most 64 MiB of HBM per device.

```python
import math
import jax
import jax.numpy as jnp
from jax import lax

C = 4096
TAPS = 128
SEQ = 8192


def draw_filter_taps(key, part):
    key = jax.random.fold_in(key, 7)
    noise_key, length_key = jax.random.split(key)
    noise_draw = jnp.clip(jax.random.normal(noise_key, (TAPS, C), jnp.float32), -4.0, 4.0)
    lowest = 16.0
    highest = 2048.0
    spread = jax.random.uniform(length_key, (1, C), jnp.float32)
    decay_length = jnp.exp(jnp.log(lowest) + spread * (jnp.log(highest) - jnp.log(lowest)))
    position = jnp.arange(TAPS, dtype=jnp.float32)[:, None]
    return 0.15 * noise_draw * jnp.exp(-position / decay_length)


def shard_levels(own_key, dims, cuts, low, largest):
    gain, own = 1.0, jax.random.fold_in(own_key, 6)
    for dim, blocks in cuts:
        draws = jnp.exp(jax.random.uniform(jax.random.fold_in(own, dim), (blocks,), jnp.float32, low / len(cuts), largest / len(cuts)))
        gain = gain * jnp.repeat(draws, dims[dim] // blocks).reshape([-1 if axis == dim else 1 for axis in range(len(dims))])
    return gain


def normal_values(own_key, dims, width, limit, cuts=(), kind=jnp.bfloat16):
    drawn = width * jax.random.normal(own_key, dims, jnp.float32)
    if cuts:
        drawn = drawn * shard_levels(own_key, dims, cuts, -0.22, 0.18)
    return jnp.clip(drawn, -limit, limit).astype(kind)


def setup_inputs(seed: int = 0) -> dict:
    seeds = jax.random.split(jax.random.key(seed), 7)
    return {
        "q_stream": normal_values(seeds[0], (SEQ, C), 1.0, 6.0, ((0, 64), (1, 8))),
        "k_stream": normal_values(seeds[1], (SEQ, C), 1.0, 6.0, ((0, 64), (1, 8))),
        "v_stream": normal_values(seeds[2], (SEQ, C), 1.0, 6.0, ((0, 64), (1, 8))),
        "filter_taps": draw_filter_taps(jax.random.fold_in(seeds[6], 71), 0),
        "short_taps": normal_values(seeds[4], (9, C), 0.6, 3.0, ((1, 8),), jnp.float32),
        "cotangent": normal_values(seeds[5], (SEQ, C), 1.0, 6.0, ((0, 64), (1, 8))),
    }


def apply_causal(signal, taps):
    tap_count = taps.shape[0]
    length = signal.shape[0]
    padded = jnp.concatenate([jnp.zeros((tap_count - 1, signal.shape[1]), signal.dtype), signal], 0)

    def accumulate(tap_index, running):
        start = (tap_count - 1 - tap_index).astype(jnp.int32)
        window = lax.dynamic_slice_in_dim(padded, start, length, 0)
        return running + lax.dynamic_index_in_dim(taps, tap_index, 0, keepdims=False) * window
    return lax.fori_loop(0, tap_count, accumulate, jnp.zeros_like(signal))

def apply_anticausal(signal, taps):
    tap_count = taps.shape[0]
    length = signal.shape[0]
    padded = jnp.concatenate([signal, jnp.zeros((tap_count - 1, signal.shape[1]), signal.dtype)], 0)

    def accumulate(tap_index, running):
        start = jnp.asarray(tap_index).astype(jnp.int32)
        window = lax.dynamic_slice_in_dim(padded, start, length, 0)
        return running + lax.dynamic_index_in_dim(taps, tap_index, 0, keepdims=False) * window
    return lax.fori_loop(0, tap_count, accumulate, jnp.zeros_like(signal))

def lag_totals(grads, signal, tap_count):
    length = signal.shape[0]
    padded = jnp.concatenate([jnp.zeros((tap_count - 1, signal.shape[1]), signal.dtype), signal], 0)

    def one_tap(tap_index):
        start = (tap_count - 1 - tap_index).astype(jnp.int32)
        window = lax.dynamic_slice_in_dim(padded, start, length, 0)
        return lax.optimization_barrier(jnp.sum(grads * window, axis=0))
    return lax.map(one_tap, jnp.arange(tap_count, dtype=jnp.int32))

def reference(q_stream, k_stream, v_stream, filter_taps, short_taps, cotangent):
    filters = filter_taps.astype(jnp.float32)
    shorts = short_taps.astype(jnp.float32)
    query_float = q_stream.astype(jnp.float32)
    key_float = k_stream.astype(jnp.float32)
    value_float = v_stream.astype(jnp.float32)
    query_act = apply_causal(query_float, shorts[0:3])
    key_act = apply_causal(key_float, shorts[3:6])
    value_act = apply_causal(value_float, shorts[6:9])
    product = key_act * value_act
    long_part = apply_causal(product, filters)
    mixed = (query_act * long_part).astype(jnp.bfloat16)
    upstream_float = cotangent.astype(jnp.float32)
    long_grad = upstream_float * query_act
    query_err = upstream_float * long_part
    product_grad = apply_anticausal(long_grad, filters)
    key_err = product_grad * value_act
    value_err = product_grad * key_act
    grad_q = apply_anticausal(query_err, shorts[0:3]).astype(jnp.bfloat16)
    grad_k = apply_anticausal(key_err, shorts[3:6]).astype(jnp.bfloat16)
    grad_v = apply_anticausal(value_err, shorts[6:9]).astype(jnp.bfloat16)
    filter_part = lag_totals(long_grad, product, TAPS)
    short_part = jnp.concatenate([lag_totals(query_err, query_float, 3), lag_totals(key_err, key_float, 3), lag_totals(value_err, value_float, 3)], 0)
    norm_factor = 1.0 / math.sqrt(SEQ)
    grad_filter = filter_part * norm_factor
    grad_short = short_part * norm_factor
    return (mixed, grad_q, grad_k, grad_v, grad_filter, grad_short)
```

```python
import functools
import math

import jax
import jax.numpy as jnp
import ml_dtypes
import numpy as np
from jax import lax
from jax.experimental import pallas as pl
from jax.experimental.pallas import tpu as pltpu
from jax.sharding import PartitionSpec as P

BF16 = jnp.bfloat16
F32 = jnp.float32

ROWS = 128
PERIOD = 256
HALF = PERIOD // 2
OUT = 136
WIDE = 256
EDGE = 16
TILE = 128
CHUNK = 24
VMEM_LIMIT = 48 * 1024 * 1024


def two_parts(matrix):
    high = matrix.astype(ml_dtypes.bfloat16)
    low = (matrix - high.astype(np.float64)).astype(ml_dtypes.bfloat16)
    return np.stack([high, low])


def transform_matrices():
    freqs = np.arange(HALF) + 0.5

    def angles(places):
        return 2.0 * np.pi * np.outer(freqs, places) / PERIOD

    forward = angles(np.arange(PERIOD))
    forward = np.concatenate([np.cos(forward), -np.sin(forward)], 0)

    def inverse(places):
        turned = angles(places).T
        return np.concatenate([np.cos(turned), -np.sin(turned)], 1) * (2.0 / PERIOD)

    long_back = inverse(np.arange(HALF, HALF + OUT))
    grad_back = inverse(np.arange(OUT))
    filter_back = inverse(HALF - np.arange(ROWS))
    return tuple(two_parts(m) for m in (forward, long_back, grad_back, filter_back))


def split(value):
    high = value.astype(BF16)
    low = (value - high.astype(F32)).astype(BF16)
    return high, low


def dot3(matrix_high, matrix_low, value):
    high, low = split(value)
    dot = functools.partial(jnp.dot, preferred_element_type=F32)
    return dot(matrix_high, high) + (dot(matrix_high, low) + dot(matrix_low, high))


def as_chunk(tile, row_value):
    first = tile.astype(BF16).astype(F32)
    row_first = row_value.astype(BF16).astype(F32)
    row = lax.broadcasted_iota(jnp.int32, (8, TILE), 0)
    last = jnp.where(row == 0, row_first, jnp.where(row == 1, row_value - row_first, 0.0))
    return jnp.concatenate([first, tile - first, last], 0).astype(BF16)


def layer_kernel(
    q_ref, k_ref, v_ref, c_ref,
    k_prev, v_prev, q_next, c_next,
    q_tail, kv_tail, kv_head, qc_head,
    h_ref, s_ref,
    fwd_ref, long_ref, grad_ref, filt_ref,
    mixed_ref, gq_ref, gk_ref, gv_ref, part_ref,
    q_ext, k_ext, v_ext, e_ext,
):
    def f32(x):
        return x.astype(F32)

    q_ext[0:8] = f32(q_tail[...])[8:16]
    q_ext[8:136] = f32(q_ref[...])
    q_ext[136:264] = f32(q_next[...])
    q_ext[264:272] = f32(qc_head[0:EDGE])[0:8]
    for ext, own, prev, n in ((k_ext, k_ref, k_prev, 0), (v_ext, v_ref, v_prev, 1)):
        ext[0:8] = f32(kv_tail[EDGE * n : EDGE * (n + 1)])[8:16]
        ext[8:136] = f32(prev[...])
        ext[136:264] = f32(own[...])
        ext[264:272] = f32(kv_head[EDGE * n : EDGE * (n + 1)])[0:8]

    def tap(s, j):
        return s_ref[3 * s + j : 3 * s + j + 1, :]

    def causal(ext, s):
        return (
            tap(s, 0) * ext[8:272] + tap(s, 1) * ext[7:271] + tap(s, 2) * ext[6:270]
        )

    a0 = causal(q_ext, 0)
    a1 = causal(k_ext, 1)
    a2 = causal(v_ext, 2)
    product = a1 * a2
    cot = f32(c_ref[...])
    cot_next = f32(c_next[...])
    cot_far = f32(qc_head[EDGE : 2 * EDGE])[0:8]
    lg_own = cot * a0[0:128]
    lg_next = cot_next * a0[128:256]
    lg_far = cot_far * a0[256:264]

    taps = h_ref[...]
    fh, fl = fwd_ref[0], fwd_ref[1]
    x_f = dot3(fh, fl, product[0:256])
    own_f = dot3(fh[:, 0:128], fl[:, 0:128], lg_own)
    lg_f = own_f + dot3(fh[:, 128:256], fl[:, 128:256], lg_next)
    h_f = dot3(fh[:, 0:128], fl[:, 0:128], taps)

    def times(a, b):
        ar, ai, br, bi = a[0:128], a[128:256], b[0:128], b[128:256]
        return jnp.concatenate([ar * br - ai * bi, ar * bi + ai * br], 0)

    def times_conj(a, b):
        ar, ai, br, bi = a[0:128], a[128:256], b[0:128], b[128:256]
        return jnp.concatenate([ar * br + ai * bi, ai * br - ar * bi], 0)

    long = dot3(long_ref[0], long_ref[1], times(x_f, h_f))
    pg = dot3(grad_ref[0], grad_ref[1], times_conj(lg_f, h_f))
    filt = dot3(filt_ref[0], filt_ref[1], times_conj(x_f, own_f))

    h0, h1, h127 = taps[0:1], taps[1:2], taps[127:128]
    p_first = product[0:8]
    p_last = product[256:264]
    row = lax.broadcasted_iota(jnp.int32, (8, long.shape[1]), 0)
    sum0 = p_last[0:1] + p_first[0:1]
    sum1 = p_last[1:2] + p_first[1:2]
    fix_long = jnp.where(row == 0, h0 * sum0, jnp.where(row == 1, h0 * sum1 + h1 * sum0, 0.0))
    fix_grad = jnp.where(row == 1, h127 * (lg_far[0:1] + lg_own[0:1]), 0.0)
    long_own, long_far = long[0:128], long[128:136] + fix_long
    pg_own, pg_far = pg[0:128], pg[128:136] + fix_grad

    mixed_ref[...] = (a0[0:128] * long_own).astype(BF16)

    short = []

    def finish(s, err_own, err_far, ext, base, out_ref):
        e_ext[0:128] = err_own
        e_ext[128:136] = err_far
        total = tap(s, 0) * err_own + tap(s, 1) * e_ext[1:129] + tap(s, 2) * e_ext[2:130]
        out_ref[...] = total.astype(BF16)
        for j in range(3):
            short.append(
                jnp.sum(err_own * ext[base - j : base - j + 128], axis=0, keepdims=True)
            )

    finish(0, cot * long_own, cot_next[0:8] * long_far, q_ext, 8, gq_ref)
    finish(1, pg_own * a2[128:256], pg_far * a2[256:264], k_ext, 136, gk_ref)
    finish(2, pg_own * a1[128:256], pg_far * a1[256:264], v_ext, 136, gv_ref)

    for h in range(WIDE // TILE):
        cols = slice(h * TILE, (h + 1) * TILE)
        for g in range(16):
            row_value = short[g][:, cols] if g < 9 else jnp.zeros((1, TILE), F32)
            part_ref[h, g] = as_chunk(filt[8 * g : 8 * g + 8, cols], row_value)


def run_layer(args, taps, shorts, matrices):
    channels = args[0].shape[1]
    steps = channels // WIDE

    def rows(count):
        return pl.BlockSpec((count, WIDE), lambda i: (0, i))

    def whole(matrix):
        return pl.BlockSpec(matrix.shape, lambda i: (0, 0, 0))

    sizes = [ROWS] * 8 + [EDGE, 2 * EDGE, 2 * EDGE, 2 * EDGE] + [ROWS, 9]
    out_rows = jax.ShapeDtypeStruct((ROWS, channels), BF16)
    ext = pltpu.VMEM((272, WIDE), F32)
    return pl.pallas_call(
        layer_kernel,
        grid=(steps,),
        in_specs=[rows(n) for n in sizes] + [whole(m) for m in matrices],
        out_specs=[rows(ROWS)] * 4
        + [pl.BlockSpec((WIDE // TILE, 16, CHUNK, TILE), lambda i: (i, 0, 0, 0))],
        out_shape=[out_rows] * 4
        + [jax.ShapeDtypeStruct((channels // TILE, 16, CHUNK, TILE), BF16)],
        scratch_shapes=[ext, ext, ext, pltpu.VMEM((OUT, WIDE), F32)],
        compiler_params=pltpu.CompilerParams(vmem_limit_bytes=VMEM_LIMIT),
        name="layer",
    )(*args, taps, shorts, *matrices)


def sum_kernel(part_ref, tile_ref, short_ref):
    total = jnp.sum(part_ref[...].astype(F32), axis=0)
    tile_ref[...] = total[0:8] + total[8:16]
    short_ref[...] = jnp.broadcast_to(total[16:17] + total[17:18], (8, TILE))


def spread_kernel(tile_ref, short_ref, out_ref):
    chunk = as_chunk(tile_ref[...], short_ref[0:1])
    out_ref[...] = jnp.broadcast_to(chunk[None], out_ref.shape)


def final_kernel(scale, groups, gathered_ref, filter_ref, short_ref):
    for h in range(4):
        for d in range(groups):
            for half in range(2):
                chunk = gathered_ref[h * 16 + d * 2 + half].astype(F32)
                start = (d * 4 + h) * TILE
                filter_ref[8 * half : 8 * half + 8, start : start + TILE] = (
                    chunk[0:8] + chunk[8:16]
                ) * scale
        for g in range(9):
            chunk = gathered_ref[h * 16 + g].astype(F32)
            short_ref[g : g + 1, h * TILE : (h + 1) * TILE] = (
                chunk[16:17] + chunk[17:18]
            ) * scale


def on_device(q_stream, k_stream, v_stream, filter_taps, short_taps, cotangent, *, matrices):
    groups, peers = lax.axis_size("dp"), lax.axis_size("ctx")

    def shifted(value, by):
        pairs = [(i, i + by) for i in range(peers) if 0 <= i + by < peers]
        return lax.ppermute(value, "ctx", pairs)

    k_prev = shifted(k_stream, 1)
    v_prev = shifted(v_stream, 1)
    q_next = shifted(q_stream, -1)
    c_next = shifted(cotangent, -1)
    q_tail = shifted(q_stream[ROWS - EDGE :], 1)
    kv_tail = shifted(jnp.concatenate([k_stream[ROWS - EDGE :], v_stream[ROWS - EDGE :]], 0), 2)
    kv_head = shifted(jnp.concatenate([k_stream[:EDGE], v_stream[:EDGE]], 0), -1)
    qc_head = shifted(jnp.concatenate([q_stream[:EDGE], cotangent[:EDGE]], 0), -2)
    taps = lax.all_to_all(filter_taps, "dp", split_axis=1, concat_axis=0, tiled=True)

    mixed, grad_q, grad_k, grad_v, part = run_layer(
        (
            q_stream, k_stream, v_stream, cotangent,
            k_prev, v_prev, q_next, c_next,
            q_tail, kv_tail, kv_head, qc_head,
        ),
        taps,
        short_taps,
        matrices,
    )

    part = part.reshape(peers, CHUNK, TILE)
    part = lax.all_to_all(part, "ctx", split_axis=0, concat_axis=0, tiled=True)
    tile, short = pl.pallas_call(
        sum_kernel,
        out_shape=[
            jax.ShapeDtypeStruct((8, TILE), F32),
            jax.ShapeDtypeStruct((8, TILE), F32),
        ],
        name="sum",
    )(part)

    pairs = [
        (d * peers + h * 16 + e * 2 + half, e * peers + h * 16 + d * 2 + half)
        for d in range(groups)
        for h in range(4)
        for e in range(groups)
        for half in range(2)
    ]
    tile = lax.ppermute(tile, ("dp", "ctx"), pairs)
    sent = pl.pallas_call(
        spread_kernel,
        out_shape=jax.ShapeDtypeStruct((peers, CHUNK, TILE), BF16),
        name="spread",
    )(tile, short)
    gathered = lax.all_to_all(sent, "ctx", split_axis=0, concat_axis=0, tiled=True)
    scale = 1.0 / math.sqrt(ROWS * peers)
    grad_filter, grad_short = pl.pallas_call(
        functools.partial(final_kernel, scale, groups),
        out_shape=[
            jax.ShapeDtypeStruct(filter_taps.shape, F32),
            jax.ShapeDtypeStruct(short_taps.shape, F32),
        ],
        name="final",
    )(gathered)
    return (mixed, grad_q, grad_k, grad_v, grad_filter, grad_short)


def solution(mesh):
    streams = P("ctx", "dp")
    in_specs = (streams, streams, streams, P("dp", None), P(None, "dp"), streams)
    out_specs = (streams,) * 4 + (P("dp", None), P(None, "dp"))
    matrices = transform_matrices()
    return jax.shard_map(
        functools.partial(on_device, matrices=matrices),
        mesh=mesh,
        in_specs=in_specs,
        out_specs=out_specs,
        check_vma=False,
    )
```

```python
import functools
import math

import jax
import jax.numpy as jnp
import ml_dtypes
import numpy as np
from jax import lax
from jax.experimental import pallas as pl
from jax.experimental.pallas import tpu as pltpu
from jax.sharding import PartitionSpec as P

BF16 = jnp.bfloat16
F32 = jnp.float32

ROWS = 128
PERIOD = 256
HALF = PERIOD // 2
OUT = 136
WIDE = 256
EDGE = 16
TILE = 128
CHUNK = 24
VMEM_LIMIT = 48 * 1024 * 1024


def two_parts(matrix):
    high = matrix.astype(ml_dtypes.bfloat16)
    low = (matrix - high.astype(np.float64)).astype(ml_dtypes.bfloat16)
    return np.stack([high, low])


def transform_matrices():
    freqs = np.arange(HALF) + 0.5

    def angles(places):
        return 2.0 * np.pi * np.outer(freqs, places) / PERIOD

    forward = angles(np.arange(PERIOD))
    forward = np.concatenate([np.cos(forward), -np.sin(forward)], 0)

    def inverse(places):
        turned = angles(places).T
        return np.concatenate([np.cos(turned), -np.sin(turned)], 1) * (2.0 / PERIOD)

    long_back = inverse(np.arange(HALF, HALF + OUT))
    grad_back = inverse(np.arange(OUT))
    return tuple(two_parts(m) for m in (forward, long_back, grad_back))


def split(value):
    high = value.astype(BF16)
    low = (value - high.astype(F32)).astype(BF16)
    return high, low


def dot3(matrix_high, matrix_low, value):
    high, low = split(value)
    dot = functools.partial(jnp.dot, preferred_element_type=F32)
    return dot(matrix_high, high) + (dot(matrix_high, low) + dot(matrix_low, high))


def last_rows(row_value, others):
    first = row_value.astype(BF16).astype(F32)
    row = lax.broadcasted_iota(jnp.int32, (8, TILE), 0)
    return jnp.where(row == 0, first, jnp.where(row == 1, row_value - first, others))


def as_chunk(tile, last):
    first = tile.astype(BF16).astype(F32)
    return jnp.concatenate([first, tile - first, last], 0).astype(BF16)


def pack_kernel(q_ref, k_ref, v_ref, c_ref, right_ref, left_ref, sems):
    tail, head = pl.ds(ROWS - EDGE, EDGE), pl.ds(0, EDGE)
    moves = [
        (k_ref, right_ref.at[pl.ds(0, ROWS)]),
        (v_ref, right_ref.at[pl.ds(ROWS, ROWS)]),
        (q_ref.at[tail], right_ref.at[pl.ds(2 * ROWS, EDGE)]),
        (q_ref, left_ref.at[pl.ds(0, ROWS)]),
        (c_ref, left_ref.at[pl.ds(ROWS, ROWS)]),
        (k_ref.at[head], left_ref.at[pl.ds(2 * ROWS, EDGE)]),
        (v_ref.at[head], left_ref.at[pl.ds(2 * ROWS + EDGE, EDGE)]),
    ]
    copies = [pltpu.make_async_copy(a, b, sems.at[i]) for i, (a, b) in enumerate(moves)]
    for copy in copies:
        copy.start()
    for copy in copies:
        copy.wait()


def pack(q_stream, k_stream, v_stream, cotangent):
    channels = q_stream.shape[1]
    anywhere = pl.BlockSpec(memory_space=pl.ANY)
    return pl.pallas_call(
        pack_kernel,
        in_specs=[anywhere] * 4,
        out_specs=[anywhere] * 2,
        out_shape=[
            jax.ShapeDtypeStruct((2 * ROWS + EDGE, channels), BF16),
            jax.ShapeDtypeStruct((2 * ROWS + 2 * EDGE, channels), BF16),
        ],
        scratch_shapes=[pltpu.SemaphoreType.DMA((7,))],
        name="pack",
    )(q_stream, k_stream, v_stream, cotangent)


def layer_kernel(
    place_ref,
    q_ref, k_ref, v_ref, c_ref, before_ref, after_ref,
    h_ref, s_ref, fwd_ref, long_ref, grad_ref,
    mixed_ref, gq_ref, gk_ref, gv_ref, part_ref, fix_ref,
    q_ext, k_ext, v_ext, e_ext, filt_all, late_all, short_all,
):
    def f32(x):
        return x.astype(F32)

    fh, fl = fwd_ref[0], fwd_ref[1]
    fh_half, fl_half = fh[:, 0:HALF], fl[:, 0:HALF]
    freq = lax.broadcasted_iota(jnp.int32, (HALF, WIDE), 0)
    sign = jnp.where(freq % 2 == 0, 1.0, -1.0).astype(F32)
    row = lax.broadcasted_iota(jnp.int32, (8, WIDE), 0)

    def times(a, b):
        ar, ai, br, bi = a[0:HALF], a[HALF:], b[0:HALF], b[HALF:]
        return jnp.concatenate([ar * br - ai * bi, ar * bi + ai * br], 0)

    def times_conj(a, b):
        ar, ai, br, bi = a[0:HALF], a[HALF:], b[0:HALF], b[HALF:]
        return jnp.concatenate([ar * br + ai * bi, ai * br - ar * bi], 0)

    for step in range(q_ref.shape[1] // WIDE):
        cols = pl.ds(step * WIDE, WIDE)

        q_ext[0:8] = f32(before_ref[2 * ROWS : 2 * ROWS + EDGE, cols])[8:16]
        q_ext[8:136] = f32(q_ref[:, cols])
        q_ext[136:264] = f32(after_ref[0:ROWS, cols])
        for n, ext, own in ((0, k_ext, k_ref), (1, v_ext, v_ref)):
            ext[0:8] = jnp.zeros((8, WIDE), F32)
            ext[8:136] = f32(before_ref[ROWS * n : ROWS * (n + 1), cols])
            ext[136:264] = f32(own[:, cols])
            start = 2 * ROWS + EDGE * n
            ext[264:272] = f32(after_ref[start : start + EDGE, cols])[0:8]

        def tap(s, j):
            return s_ref[3 * s + j : 3 * s + j + 1, cols]

        def causal(ext, s, count):
            return (
                tap(s, 0) * ext[8 : 8 + count]
                + tap(s, 1) * ext[7 : 7 + count]
                + tap(s, 2) * ext[6 : 6 + count]
            )

        a0 = causal(q_ext, 0, 256)
        a1 = causal(k_ext, 1, 264)
        a2 = causal(v_ext, 2, 264)
        product = a1 * a2
        p_before = jnp.concatenate([jnp.where(row < 2, 0.0, product[0:8]), product[8:128]], 0)
        p_own, p_far = product[128:256], product[256:264]
        cot = f32(c_ref[:, cols])
        cot_next = f32(after_ref[ROWS : 2 * ROWS, cols])
        lg = jnp.concatenate([cot, cot_next], 0) * a0

        taps = h_ref[:, cols]
        own_f = dot3(fh_half, fl_half, p_own)
        before_f = dot3(fh_half, fl_half, p_before)
        moved_f = jnp.concatenate([own_f[HALF:] * sign, own_f[0:HALF] * -sign], 0)
        x_f = before_f + moved_f
        lg_f = dot3(fh, fl, lg)
        h_f = dot3(fh_half, fl_half, taps)

        long = dot3(long_ref[0], long_ref[1], times(x_f, h_f))
        pg = dot3(grad_ref[0], grad_ref[1], times_conj(lg_f, h_f))
        filt_all[:, cols] = dot3(grad_ref[0, 0:ROWS], grad_ref[1, 0:ROWS], times_conj(lg_f, own_f))

        h0, h1, h127 = taps[0:1], taps[1:2], taps[127:128]
        p0, p1 = p_far[0:1], p_far[1:2]
        fix_long = jnp.where(row == 0, h0 * p0, jnp.where(row == 1, h0 * p1 + h1 * p0, 0.0))
        fix_grad = jnp.where(row == 1, h127 * lg[0:1], 0.0)
        long_own, long_far = long[0:128], long[128:136] + fix_long
        pg_own, pg_far = pg[0:128], pg[128:136] + fix_grad

        mixed = a0[0:128] * long_own
        mixed_ref[:, cols] = mixed.astype(BF16)

        def finish(s, err_own, err_far, ext, base, out_ref):
            e_ext[0:128] = err_own
            e_ext[128:136] = err_far
            total = tap(s, 0) * err_own + tap(s, 1) * e_ext[1:129] + tap(s, 2) * e_ext[2:130]
            out_ref[:, cols] = total.astype(BF16)
            for j in range(3):
                short_all[3 * s + j : 3 * s + j + 1, cols] = jnp.sum(
                    err_own * ext[base - j : base - j + 128], axis=0, keepdims=True
                )
            return total

        gq = finish(0, cot * long_own, cot_next[0:8] * long_far, q_ext, 8, gq_ref)
        gk = finish(1, pg_own * a2[128:256], pg_far * a2[256:264], k_ext, 136, gk_ref)
        gv = finish(2, pg_own * a1[128:256], pg_far * a1[256:264], v_ext, 136, gv_ref)
        lacking = cot_next[0:1] * h127 * p_own[1:2]
        for j in range(3):
            short_all[j : j + 1, cols] += lacking * q_ext[136 - j : 137 - j]

        late_all[0:1, cols] = p_own[1:2]
        late_all[1:2, cols] = lg[128:129]
        fix_ref[0:1, cols] = mixed[0:1]
        fix_ref[1:2, cols] = gq[0:1]
        fix_ref[2:3, cols] = gk[127:128]
        fix_ref[3:4, cols] = gv[127:128]
        fix_ref[4:5, cols] = a0[0:1] * h127
        fix_ref[5:6, cols] = tap(0, 0) * cot[0:1] * h127
        fix_ref[6:7, cols] = tap(1, 2) * h127 * a2[257:258]
        fix_ref[7:8, cols] = tap(2, 2) * h127 * a1[257:258]

    place = place_ref[0]
    row = lax.broadcasted_iota(jnp.int32, (8, TILE), 0)
    late = []
    for n in range(2):
        rows = jnp.zeros((8, TILE), F32)
        for h in range(4):
            value = late_all[n : n + 1, h * TILE : (h + 1) * TILE]
            rows = jnp.where(row == 2 + h, value, rows)
        late.append(rows)
    for m in range(4):
        to_right = lax.rem(m + 64 - place, 4) == 1
        others = jnp.where(to_right, late[0], late[1])
        for g in range(m, 16, 4):
            for h in range(4):
                lanes = slice(h * TILE, (h + 1) * TILE)
                value = short_all[g : g + 1, lanes] if g < 9 else jnp.zeros((1, TILE), F32)
                part_ref[16 * h + g] = as_chunk(
                    filt_all[8 * g : 8 * g + 8, lanes], last_rows(value, others)
                )


def run_layer(place, streams, before, after, taps, shorts, matrices):
    channels = streams[0].shape[1]
    out_rows = jax.ShapeDtypeStruct((ROWS, channels), BF16)
    ext = pltpu.VMEM((272, WIDE), F32)
    vmem = pl.BlockSpec(memory_space=pltpu.VMEM)
    return pl.pallas_call(
        layer_kernel,
        in_specs=[pl.BlockSpec(memory_space=pltpu.SMEM)] + [vmem] * 11,
        out_specs=[vmem] * 6,
        out_shape=[out_rows] * 4
        + [
            jax.ShapeDtypeStruct((64, CHUNK, TILE), BF16),
            jax.ShapeDtypeStruct((8, channels), F32),
        ],
        scratch_shapes=[
            ext, ext, ext,
            pltpu.VMEM((OUT, WIDE), F32),
            pltpu.VMEM((ROWS, channels), F32),
            pltpu.VMEM((8, channels), F32),
            pltpu.VMEM((16, channels), F32),
        ],
        compiler_params=pltpu.CompilerParams(vmem_limit_bytes=VMEM_LIMIT),
        name="layer",
    )(place, *streams, before, after, taps, shorts, *matrices)


def sum_kernel(place_ref, part_ref, tile_ref, short_ref, late_ref):
    total = jnp.sum(part_ref[:, 0:EDGE].astype(F32), axis=0)
    tile_ref[...] = total[0:8] + total[8:16]
    total = jnp.sum(part_ref[:, EDGE:CHUNK].astype(F32), axis=0)
    short_ref[...] = jnp.broadcast_to(total[0:1] + total[1:2], (8, TILE))
    place, peers = place_ref[0], part_ref.shape[0]
    before = part_ref[jnp.maximum(place - 1, 0), EDGE:CHUNK].astype(F32)
    after = part_ref[jnp.minimum(place + 1, peers - 1), EDGE:CHUNK].astype(F32)
    late_ref[0:8] = jnp.where(place > 0, before, 0.0)
    late_ref[8:16] = jnp.where(place < peers - 1, after, 0.0)


def patch_kernel(late_ref, fix_ref, mixed_in, gq_in, gk_in, gv_in, mixed_ref, gq_ref, gk_ref, gv_ref):
    row = lax.broadcasted_iota(jnp.int32, (EDGE, TILE), 0)
    plan = (
        (0, 0, 0, mixed_in, mixed_ref),
        (1, 0, 0, gq_in, gq_ref),
        (2, 8, EDGE - 1, gk_in, gk_ref),
        (3, 8, EDGE - 1, gv_in, gv_ref),
    )
    for n, source, place, old_ref, new_ref in plan:
        for h in range(old_ref.shape[1] // TILE):
            lanes = slice(h * TILE, (h + 1) * TILE)
            late = late_ref[source + 2 + h : source + 3 + h]
            value = fix_ref[n : n + 1, lanes] + fix_ref[4 + n : 5 + n, lanes] * late
            old = old_ref[:, lanes].astype(F32)
            new_ref[:, lanes] = jnp.where(row == place, value, old).astype(BF16)


def patch(late, fix, outs):
    channels = outs[0].shape[1]

    def edge(block):
        return pl.BlockSpec((EDGE, channels), lambda i: (block, 0))

    edges = [edge(0), edge(0), edge(ROWS // EDGE - 1), edge(ROWS // EDGE - 1)]
    return pl.pallas_call(
        patch_kernel,
        grid=(1,),
        in_specs=[
            pl.BlockSpec(late.shape, lambda i: (0, 0)),
            pl.BlockSpec(fix.shape, lambda i: (0, 0)),
        ]
        + edges,
        out_specs=edges,
        out_shape=[jax.ShapeDtypeStruct(o.shape, o.dtype) for o in outs],
        input_output_aliases={2: 0, 3: 1, 4: 2, 5: 3},
        name="patch",
    )(late, fix, *outs)


def spread_kernel(tile_ref, short_ref, out_ref):
    chunk = as_chunk(tile_ref[...], last_rows(short_ref[0:1], jnp.zeros((8, TILE), F32)))
    out_ref[...] = jnp.broadcast_to(chunk[None], out_ref.shape)


def final_kernel(scale, groups, gathered_ref, filter_ref, short_ref):
    for h in range(4):
        for d in range(groups):
            for half in range(2):
                chunk = gathered_ref[h * 16 + d * 2 + half].astype(F32)
                start = (d * 4 + h) * TILE
                filter_ref[8 * half : 8 * half + 8, start : start + TILE] = (
                    chunk[0:8] + chunk[8:16]
                ) * scale
        for g in range(9):
            chunk = gathered_ref[h * 16 + g].astype(F32)
            short_ref[g : g + 1, h * TILE : (h + 1) * TILE] = (
                chunk[16:17] + chunk[17:18]
            ) * scale


def on_device(q_stream, k_stream, v_stream, filter_taps, short_taps, cotangent, *, matrices):
    groups, peers = lax.axis_size("dp"), lax.axis_size("ctx")

    def shifted(value, by):
        pairs = [(i, i + by) for i in range(peers) if 0 <= i + by < peers]
        return lax.ppermute(value, "ctx", pairs)

    right, left = pack(q_stream, k_stream, v_stream, cotangent)
    before = shifted(right, 1)
    after = shifted(left, -1)
    taps = lax.all_to_all(filter_taps, "dp", split_axis=1, concat_axis=0, tiled=True)
    place = lax.axis_index("ctx").astype(jnp.int32).reshape(1)

    *outs, part, fix = run_layer(
        place,
        (q_stream, k_stream, v_stream, cotangent),
        before,
        after,
        taps,
        short_taps,
        matrices,
    )

    part = lax.all_to_all(part, "ctx", split_axis=0, concat_axis=0, tiled=True)
    vmem = pl.BlockSpec(memory_space=pltpu.VMEM)
    tile, short, late = pl.pallas_call(
        sum_kernel,
        in_specs=[pl.BlockSpec(memory_space=pltpu.SMEM), vmem],
        out_specs=[vmem] * 3,
        out_shape=[
            jax.ShapeDtypeStruct((8, TILE), F32),
            jax.ShapeDtypeStruct((8, TILE), F32),
            jax.ShapeDtypeStruct((EDGE, TILE), F32),
        ],
        name="sum",
    )(place, part)

    pairs = [
        (d * peers + h * 16 + e * 2 + half, e * peers + h * 16 + d * 2 + half)
        for d in range(groups)
        for h in range(4)
        for e in range(groups)
        for half in range(2)
    ]
    tile = lax.ppermute(tile, ("dp", "ctx"), pairs)
    sent = pl.pallas_call(
        spread_kernel,
        out_shape=jax.ShapeDtypeStruct((peers, CHUNK, TILE), BF16),
        name="spread",
    )(tile, short)
    outs = patch(late, fix, outs)
    gathered = lax.all_to_all(sent, "ctx", split_axis=0, concat_axis=0, tiled=True)
    scale = 1.0 / math.sqrt(ROWS * peers)
    grad_filter, grad_short = pl.pallas_call(
        functools.partial(final_kernel, scale, groups),
        out_shape=[
            jax.ShapeDtypeStruct(filter_taps.shape, F32),
            jax.ShapeDtypeStruct(short_taps.shape, F32),
        ],
        name="final",
    )(gathered)
    return (*outs, grad_filter, grad_short)


def solution(mesh):
    streams = P("ctx", "dp")
    in_specs = (streams, streams, streams, P("dp", None), P(None, "dp"), streams)
    out_specs = (streams,) * 4 + (P("dp", None), P(None, "dp"))
    matrices = transform_matrices()
    return jax.shard_map(
        functools.partial(on_device, matrices=matrices),
        mesh=mesh,
        in_specs=in_specs,
        out_specs=out_specs,
        check_vma=False,
    )
```

```python
import functools
import math

import jax
import jax.numpy as jnp
import ml_dtypes
import numpy as np
from jax import lax
from jax.experimental import pallas as pl
from jax.experimental.pallas import tpu as pltpu
from jax.sharding import PartitionSpec as P

BF16 = jnp.bfloat16
F32 = jnp.float32

ROWS = 128
PERIOD = 256
HALF = PERIOD // 2
OUT = 136
WIDE = 256
EDGE = 16
TILE = 128
CHUNK = 24
VMEM_LIMIT = 48 * 1024 * 1024


def two_parts(matrix):
    high = matrix.astype(ml_dtypes.bfloat16)
    low = (matrix - high.astype(np.float64)).astype(ml_dtypes.bfloat16)
    return np.stack([high, low])


def transform_matrices():
    freqs = np.arange(HALF) + 0.5

    def angles(places):
        return 2.0 * np.pi * np.outer(freqs, places) / PERIOD

    forward = angles(np.arange(PERIOD))
    forward = np.concatenate([np.cos(forward), -np.sin(forward)], 0)

    def inverse(places):
        turned = angles(places).T
        return np.concatenate([np.cos(turned), -np.sin(turned)], 1) * (2.0 / PERIOD)

    long_back = inverse(np.arange(HALF, HALF + OUT))
    grad_back = inverse(np.arange(OUT))
    return tuple(two_parts(m) for m in (forward, long_back, grad_back))


def split(value):
    high = value.astype(BF16)
    low = (value - high.astype(F32)).astype(BF16)
    return high, low


def dot3(matrix_high, matrix_low, value):
    high, low = split(value)
    dot = functools.partial(jnp.dot, preferred_element_type=F32)
    return dot(matrix_high, high) + (dot(matrix_high, low) + dot(matrix_low, high))


def last_rows(row_value, others):
    first = row_value.astype(BF16).astype(F32)
    row = lax.broadcasted_iota(jnp.int32, (8, TILE), 0)
    return jnp.where(row == 0, first, jnp.where(row == 1, row_value - first, others))


def as_chunk(tile, last):
    first = tile.astype(BF16).astype(F32)
    return jnp.concatenate([first, tile - first, last], 0).astype(BF16)


def pack_kernel(q_ref, k_ref, v_ref, c_ref, right_ref, left_ref):
    tail, head = pl.ds(ROWS - EDGE, EDGE), pl.ds(0, EDGE)
    right_ref[0:ROWS] = k_ref[...]
    right_ref[ROWS : 2 * ROWS] = v_ref[...]
    right_ref[2 * ROWS : 2 * ROWS + EDGE] = q_ref[tail]
    left_ref[0:ROWS] = q_ref[...]
    left_ref[ROWS : 2 * ROWS] = c_ref[...]
    left_ref[2 * ROWS : 2 * ROWS + EDGE] = k_ref[head]
    left_ref[2 * ROWS + EDGE : 2 * ROWS + 2 * EDGE] = v_ref[head]


def pack(q_stream, k_stream, v_stream, cotangent):
    channels = q_stream.shape[1]
    vmem = pl.BlockSpec(memory_space=pltpu.VMEM)
    return pl.pallas_call(
        pack_kernel,
        in_specs=[vmem] * 4,
        out_specs=[vmem] * 2,
        out_shape=[
            jax.ShapeDtypeStruct((2 * ROWS + EDGE, channels), BF16),
            jax.ShapeDtypeStruct((2 * ROWS + 2 * EDGE, channels), BF16),
        ],
        name="pack",
    )(q_stream, k_stream, v_stream, cotangent)


def layer_kernel(
    place_ref,
    q_ref, k_ref, v_ref, c_ref, before_ref, after_ref,
    h_ref, s_ref, fwd_ref, long_ref, grad_ref,
    mixed_ref, gq_ref, gk_ref, gv_ref, part_ref, fix_ref,
    q_ext, k_ext, v_ext, e_ext, filt_all, late_all, short_all,
):
    def f32(x):
        return x.astype(F32)

    fh, fl = fwd_ref[0], fwd_ref[1]
    fh_half, fl_half = fh[:, 0:HALF], fl[:, 0:HALF]
    freq = lax.broadcasted_iota(jnp.int32, (HALF, WIDE), 0)
    sign = jnp.where(freq % 2 == 0, 1.0, -1.0).astype(F32)
    row = lax.broadcasted_iota(jnp.int32, (8, WIDE), 0)

    def times(a, b):
        ar, ai, br, bi = a[0:HALF], a[HALF:], b[0:HALF], b[HALF:]
        return jnp.concatenate([ar * br - ai * bi, ar * bi + ai * br], 0)

    def times_conj(a, b):
        ar, ai, br, bi = a[0:HALF], a[HALF:], b[0:HALF], b[HALF:]
        return jnp.concatenate([ar * br + ai * bi, ai * br - ar * bi], 0)

    for step in range(q_ref.shape[1] // WIDE):
        cols = pl.ds(step * WIDE, WIDE)

        q_ext[0:8] = f32(before_ref[2 * ROWS : 2 * ROWS + EDGE, cols])[8:16]
        q_ext[8:136] = f32(q_ref[:, cols])
        q_ext[136:264] = f32(after_ref[0:ROWS, cols])
        for n, ext, own in ((0, k_ext, k_ref), (1, v_ext, v_ref)):
            ext[0:8] = jnp.zeros((8, WIDE), F32)
            ext[8:136] = f32(before_ref[ROWS * n : ROWS * (n + 1), cols])
            ext[136:264] = f32(own[:, cols])
            start = 2 * ROWS + EDGE * n
            ext[264:272] = f32(after_ref[start : start + EDGE, cols])[0:8]

        def tap(s, j):
            return s_ref[3 * s + j : 3 * s + j + 1, cols]

        def causal(ext, s, count):
            return (
                tap(s, 0) * ext[8 : 8 + count]
                + tap(s, 1) * ext[7 : 7 + count]
                + tap(s, 2) * ext[6 : 6 + count]
            )

        a0 = causal(q_ext, 0, 256)
        a1 = causal(k_ext, 1, 264)
        a2 = causal(v_ext, 2, 264)
        product = a1 * a2
        p_before = jnp.concatenate([jnp.where(row < 2, 0.0, product[0:8]), product[8:128]], 0)
        p_own, p_far = product[128:256], product[256:264]
        cot = f32(c_ref[:, cols])
        cot_next = f32(after_ref[ROWS : 2 * ROWS, cols])
        lg = jnp.concatenate([cot, cot_next], 0) * a0

        taps = h_ref[:, cols]
        own_f = dot3(fh_half, fl_half, p_own)
        before_f = dot3(fh_half, fl_half, p_before)
        moved_f = jnp.concatenate([own_f[HALF:] * sign, own_f[0:HALF] * -sign], 0)
        x_f = before_f + moved_f
        lg_f = dot3(fh, fl, lg)
        h_f = dot3(fh_half, fl_half, taps)

        long = dot3(long_ref[0], long_ref[1], times(x_f, h_f))
        pg = dot3(grad_ref[0], grad_ref[1], times_conj(lg_f, h_f))
        filt_all[:, cols] = dot3(grad_ref[0, 0:ROWS], grad_ref[1, 0:ROWS], times_conj(lg_f, own_f))

        h0, h1, h127 = taps[0:1], taps[1:2], taps[127:128]
        p0, p1 = p_far[0:1], p_far[1:2]
        fix_long = jnp.where(row == 0, h0 * p0, jnp.where(row == 1, h0 * p1 + h1 * p0, 0.0))
        fix_grad = jnp.where(row == 1, h127 * lg[0:1], 0.0)
        long_own, long_far = long[0:128], long[128:136] + fix_long
        pg_own, pg_far = pg[0:128], pg[128:136] + fix_grad

        mixed = a0[0:128] * long_own
        mixed_ref[:, cols] = mixed.astype(BF16)

        def finish(s, err_own, err_far, ext, base, out_ref):
            e_ext[0:128] = err_own
            e_ext[128:136] = err_far
            total = tap(s, 0) * err_own + tap(s, 1) * e_ext[1:129] + tap(s, 2) * e_ext[2:130]
            out_ref[:, cols] = total.astype(BF16)
            for j in range(3):
                short_all[3 * s + j : 3 * s + j + 1, cols] = jnp.sum(
                    err_own * ext[base - j : base - j + 128], axis=0, keepdims=True
                )
            return total

        gq = finish(0, cot * long_own, cot_next[0:8] * long_far, q_ext, 8, gq_ref)
        gk = finish(1, pg_own * a2[128:256], pg_far * a2[256:264], k_ext, 136, gk_ref)
        gv = finish(2, pg_own * a1[128:256], pg_far * a1[256:264], v_ext, 136, gv_ref)
        lacking = cot_next[0:1] * h127 * p_own[1:2]
        for j in range(3):
            short_all[j : j + 1, cols] += lacking * q_ext[136 - j : 137 - j]

        late_all[0:1, cols] = p_own[1:2]
        late_all[1:2, cols] = lg[128:129]
        fix_ref[0:1, cols] = mixed[0:1]
        fix_ref[1:2, cols] = gq[0:1]
        fix_ref[2:3, cols] = gk[127:128]
        fix_ref[3:4, cols] = gv[127:128]
        fix_ref[4:5, cols] = a0[0:1] * h127
        fix_ref[5:6, cols] = tap(0, 0) * cot[0:1] * h127
        fix_ref[6:7, cols] = tap(1, 2) * h127 * a2[257:258]
        fix_ref[7:8, cols] = tap(2, 2) * h127 * a1[257:258]

    place = place_ref[0]
    row = lax.broadcasted_iota(jnp.int32, (8, TILE), 0)
    late = []
    for n in range(2):
        rows = jnp.zeros((8, TILE), F32)
        for h in range(4):
            value = late_all[n : n + 1, h * TILE : (h + 1) * TILE]
            rows = jnp.where(row == 2 + h, value, rows)
        late.append(rows)
    for m in range(4):
        to_right = lax.rem(m + 64 - place, 4) == 1
        others = jnp.where(to_right, late[0], late[1])
        for g in range(m, 16, 4):
            for h in range(4):
                lanes = slice(h * TILE, (h + 1) * TILE)
                value = short_all[g : g + 1, lanes] if g < 9 else jnp.zeros((1, TILE), F32)
                part_ref[16 * h + g] = as_chunk(
                    filt_all[8 * g : 8 * g + 8, lanes], last_rows(value, others)
                )


def run_layer(place, streams, before, after, taps, shorts, matrices):
    channels = streams[0].shape[1]
    out_rows = jax.ShapeDtypeStruct((ROWS, channels), BF16)
    ext = pltpu.VMEM((272, WIDE), F32)
    vmem = pl.BlockSpec(memory_space=pltpu.VMEM)
    return pl.pallas_call(
        layer_kernel,
        in_specs=[pl.BlockSpec(memory_space=pltpu.SMEM)] + [vmem] * 11,
        out_specs=[vmem] * 6,
        out_shape=[out_rows] * 4
        + [
            jax.ShapeDtypeStruct((64, CHUNK, TILE), BF16),
            jax.ShapeDtypeStruct((8, channels), F32),
        ],
        scratch_shapes=[
            ext, ext, ext,
            pltpu.VMEM((OUT, WIDE), F32),
            pltpu.VMEM((ROWS, channels), F32),
            pltpu.VMEM((8, channels), F32),
            pltpu.VMEM((16, channels), F32),
        ],
        compiler_params=pltpu.CompilerParams(vmem_limit_bytes=VMEM_LIMIT),
        name="layer",
    )(place, *streams, before, after, taps, shorts, *matrices)


def sum_kernel(place_ref, part_ref, tile_ref, short_ref, late_ref):
    total = jnp.sum(part_ref[:, 0:EDGE].astype(F32), axis=0)
    tile_ref[...] = total[0:8] + total[8:16]
    total = jnp.sum(part_ref[:, EDGE:CHUNK].astype(F32), axis=0)
    short_ref[...] = jnp.broadcast_to(total[0:1] + total[1:2], (8, TILE))
    place, peers = place_ref[0], part_ref.shape[0]
    before = part_ref[jnp.maximum(place - 1, 0), EDGE:CHUNK].astype(F32)
    after = part_ref[jnp.minimum(place + 1, peers - 1), EDGE:CHUNK].astype(F32)
    late_ref[0:8] = jnp.where(place > 0, before, 0.0)
    late_ref[8:16] = jnp.where(place < peers - 1, after, 0.0)


def patch_kernel(late_ref, fix_ref, mixed_in, gq_in, gk_in, gv_in, mixed_ref, gq_ref, gk_ref, gv_ref):
    row = lax.broadcasted_iota(jnp.int32, (EDGE, TILE), 0)
    plan = (
        (0, 0, 0, mixed_in, mixed_ref),
        (1, 0, 0, gq_in, gq_ref),
        (2, 8, EDGE - 1, gk_in, gk_ref),
        (3, 8, EDGE - 1, gv_in, gv_ref),
    )
    for n, source, place, old_ref, new_ref in plan:
        for h in range(old_ref.shape[1] // TILE):
            lanes = slice(h * TILE, (h + 1) * TILE)
            late = late_ref[source + 2 + h : source + 3 + h]
            value = fix_ref[n : n + 1, lanes] + fix_ref[4 + n : 5 + n, lanes] * late
            old = old_ref[:, lanes].astype(F32)
            new_ref[:, lanes] = jnp.where(row == place, value, old).astype(BF16)


def patch(late, fix, outs):
    channels = outs[0].shape[1]

    def edge(block):
        return pl.BlockSpec((EDGE, channels), lambda i: (block, 0))

    edges = [edge(0), edge(0), edge(ROWS // EDGE - 1), edge(ROWS // EDGE - 1)]
    return pl.pallas_call(
        patch_kernel,
        grid=(1,),
        in_specs=[
            pl.BlockSpec(late.shape, lambda i: (0, 0)),
            pl.BlockSpec(fix.shape, lambda i: (0, 0)),
        ]
        + edges,
        out_specs=edges,
        out_shape=[jax.ShapeDtypeStruct(o.shape, o.dtype) for o in outs],
        input_output_aliases={2: 0, 3: 1, 4: 2, 5: 3},
        name="patch",
    )(late, fix, *outs)


def spread_kernel(tile_ref, short_ref, out_ref):
    chunk = as_chunk(tile_ref[...], last_rows(short_ref[0:1], jnp.zeros((8, TILE), F32)))
    out_ref[...] = jnp.broadcast_to(chunk[None], out_ref.shape)


def final_kernel(scale, groups, gathered_ref, filter_ref, short_ref):
    for h in range(4):
        for d in range(groups):
            for half in range(2):
                chunk = gathered_ref[h * 16 + d * 2 + half].astype(F32)
                start = (d * 4 + h) * TILE
                filter_ref[8 * half : 8 * half + 8, start : start + TILE] = (
                    chunk[0:8] + chunk[8:16]
                ) * scale
        for g in range(9):
            chunk = gathered_ref[h * 16 + g].astype(F32)
            short_ref[g : g + 1, h * TILE : (h + 1) * TILE] = (
                chunk[16:17] + chunk[17:18]
            ) * scale


def on_device(q_stream, k_stream, v_stream, filter_taps, short_taps, cotangent, *, matrices):
    groups, peers = lax.axis_size("dp"), lax.axis_size("ctx")

    def shifted(value, by):
        pairs = [(i, i + by) for i in range(peers) if 0 <= i + by < peers]
        return lax.ppermute(value, "ctx", pairs)

    right, left = pack(q_stream, k_stream, v_stream, cotangent)
    before = shifted(right, 1)
    after = shifted(left, -1)
    taps = lax.all_to_all(filter_taps, "dp", split_axis=1, concat_axis=0, tiled=True)
    place = lax.axis_index("ctx").astype(jnp.int32).reshape(1)

    *outs, part, fix = run_layer(
        place,
        (q_stream, k_stream, v_stream, cotangent),
        before,
        after,
        taps,
        short_taps,
        matrices,
    )

    part = lax.all_to_all(part, "ctx", split_axis=0, concat_axis=0, tiled=True)
    vmem = pl.BlockSpec(memory_space=pltpu.VMEM)
    tile, short, late = pl.pallas_call(
        sum_kernel,
        in_specs=[pl.BlockSpec(memory_space=pltpu.SMEM), vmem],
        out_specs=[vmem] * 3,
        out_shape=[
            jax.ShapeDtypeStruct((8, TILE), F32),
            jax.ShapeDtypeStruct((8, TILE), F32),
            jax.ShapeDtypeStruct((EDGE, TILE), F32),
        ],
        name="sum",
    )(place, part)

    pairs = [
        (d * peers + h * 16 + e * 2 + half, e * peers + h * 16 + d * 2 + half)
        for d in range(groups)
        for h in range(4)
        for e in range(groups)
        for half in range(2)
    ]
    tile = lax.ppermute(tile, ("dp", "ctx"), pairs)
    sent = pl.pallas_call(
        spread_kernel,
        out_shape=jax.ShapeDtypeStruct((peers, CHUNK, TILE), BF16),
        name="spread",
    )(tile, short)
    outs = patch(late, fix, outs)
    gathered = lax.all_to_all(sent, "ctx", split_axis=0, concat_axis=0, tiled=True)
    scale = 1.0 / math.sqrt(ROWS * peers)
    grad_filter, grad_short = pl.pallas_call(
        functools.partial(final_kernel, scale, groups),
        out_shape=[
            jax.ShapeDtypeStruct(filter_taps.shape, F32),
            jax.ShapeDtypeStruct(short_taps.shape, F32),
        ],
        name="final",
    )(gathered)
    return (*outs, grad_filter, grad_short)


def solution(mesh):
    streams = P("ctx", "dp")
    in_specs = (streams, streams, streams, P("dp", None), P(None, "dp"), streams)
    out_specs = (streams,) * 4 + (P("dp", None), P(None, "dp"))
    matrices = transform_matrices()
    return jax.shard_map(
        functools.partial(on_device, matrices=matrices),
        mesh=mesh,
        in_specs=in_specs,
        out_specs=out_specs,
        check_vma=False,
    )
```

```python
import functools
import math

import jax
import jax.numpy as jnp
import ml_dtypes
import numpy as np
from jax import lax
from jax.experimental import pallas as pl
from jax.experimental.pallas import tpu as pltpu
from jax.sharding import PartitionSpec as P

BF16 = jnp.bfloat16
F32 = jnp.float32

ROWS = 128
PERIOD = 256
HALF = PERIOD // 2
OUT = 136
WIDE = 256
EDGE = 16
TILE = 128
CHUNK = 9
VMEM_LIMIT = 24 * 1024 * 1024
SMALL = pltpu.CompilerParams(vmem_limit_bytes=8 * 1024 * 1024)


def two_parts(matrix):
    high = matrix.astype(ml_dtypes.bfloat16)
    low = (matrix - high.astype(np.float64)).astype(ml_dtypes.bfloat16)
    return np.stack([high, low])


def transform_matrices():
    freqs = np.arange(HALF) + 0.5

    def angles(places):
        return 2.0 * np.pi * np.outer(freqs, places) / PERIOD

    forward = angles(np.arange(PERIOD))
    forward = np.concatenate([np.cos(forward), -np.sin(forward)], 0)

    def inverse(places):
        turned = angles(places).T
        return np.concatenate([np.cos(turned), -np.sin(turned)], 1) * (2.0 / PERIOD)

    long_back = inverse(np.arange(HALF, HALF + OUT))
    grad_back = inverse(np.arange(OUT))
    return tuple(two_parts(m) for m in (forward, long_back, grad_back))


def split(value):
    high = value.astype(BF16)
    low = (value - high.astype(F32)).astype(BF16)
    return high, low


def dot3(matrix_high, matrix_low, value):
    high, low = split(value)
    dot = functools.partial(jnp.dot, preferred_element_type=F32)
    return dot(matrix_high, high) + (dot(matrix_high, low) + dot(matrix_low, high))


def pack_kernel(q_ref, k_ref, v_ref, c_ref, right_ref, left_ref):
    tail, head = pl.ds(ROWS - EDGE, EDGE), pl.ds(0, EDGE)
    right_ref[0:ROWS] = k_ref[...]
    right_ref[ROWS : 2 * ROWS] = v_ref[...]
    right_ref[2 * ROWS : 2 * ROWS + EDGE] = q_ref[tail]
    left_ref[0:ROWS] = q_ref[...]
    left_ref[ROWS : 2 * ROWS] = c_ref[...]
    left_ref[2 * ROWS : 2 * ROWS + EDGE] = k_ref[head]
    left_ref[2 * ROWS + EDGE : 2 * ROWS + 2 * EDGE] = v_ref[head]


def pack(q_stream, k_stream, v_stream, cotangent):
    channels = q_stream.shape[1]
    vmem = pl.BlockSpec(memory_space=pltpu.VMEM)
    return pl.pallas_call(
        pack_kernel,
        in_specs=[vmem] * 4,
        out_specs=[vmem] * 2,
        out_shape=[
            jax.ShapeDtypeStruct((2 * ROWS + EDGE, channels), BF16),
            jax.ShapeDtypeStruct((2 * ROWS + 2 * EDGE, channels), BF16),
        ],
        compiler_params=SMALL,
        name="pack",
    )(q_stream, k_stream, v_stream, cotangent)


def layer_kernel(
    q_ref, k_ref, v_ref, c_ref, before_ref, after_ref,
    h_ref, s_ref, fwd_ref, long_ref, grad_ref,
    mixed_ref, gq_ref, gk_ref, gv_ref, part_ref, fix_ref, late_ref,
    q_ext, k_ext, v_ext, e_ext, short_all,
):
    def f32(x):
        return x.astype(F32)

    fh, fl = fwd_ref[0], fwd_ref[1]
    fh_half, fl_half = fh[:, 0:HALF], fl[:, 0:HALF]
    freq = lax.broadcasted_iota(jnp.int32, (HALF, WIDE), 0)
    sign = jnp.where(freq % 2 == 0, 1.0, -1.0).astype(F32)
    row = lax.broadcasted_iota(jnp.int32, (8, WIDE), 0)

    def times(a, b):
        ar, ai, br, bi = a[0:HALF], a[HALF:], b[0:HALF], b[HALF:]
        return jnp.concatenate([ar * br - ai * bi, ar * bi + ai * br], 0)

    def times_conj(a, b):
        ar, ai, br, bi = a[0:HALF], a[HALF:], b[0:HALF], b[HALF:]
        return jnp.concatenate([ar * br + ai * bi, ai * br - ar * bi], 0)

    for step in range(q_ref.shape[1] // WIDE):
        cols = pl.ds(step * WIDE, WIDE)

        q_ext[0:8] = f32(before_ref[2 * ROWS : 2 * ROWS + EDGE, cols])[8:16]
        q_ext[8:136] = f32(q_ref[:, cols])
        q_ext[136:264] = f32(after_ref[0:ROWS, cols])
        for n, ext, own in ((0, k_ext, k_ref), (1, v_ext, v_ref)):
            ext[0:8] = jnp.zeros((8, WIDE), F32)
            ext[8:136] = f32(before_ref[ROWS * n : ROWS * (n + 1), cols])
            ext[136:264] = f32(own[:, cols])
            start = 2 * ROWS + EDGE * n
            ext[264:272] = f32(after_ref[start : start + EDGE, cols])[0:8]

        def tap(s, j):
            return s_ref[3 * s + j : 3 * s + j + 1, cols]

        def causal(ext, s, count):
            return (
                tap(s, 0) * ext[8 : 8 + count]
                + tap(s, 1) * ext[7 : 7 + count]
                + tap(s, 2) * ext[6 : 6 + count]
            )

        a0 = causal(q_ext, 0, 256)
        a1 = causal(k_ext, 1, 264)
        a2 = causal(v_ext, 2, 264)
        product = a1 * a2
        p_before = jnp.concatenate([jnp.where(row < 2, 0.0, product[0:8]), product[8:128]], 0)
        p_own, p_far = product[128:256], product[256:264]
        cot = f32(c_ref[:, cols])
        cot_next = f32(after_ref[ROWS : 2 * ROWS, cols])
        lg = jnp.concatenate([cot, cot_next], 0) * a0

        taps = h_ref[:, cols]
        own_f = dot3(fh_half, fl_half, p_own)
        before_f = dot3(fh_half, fl_half, p_before)
        moved_f = jnp.concatenate([own_f[HALF:] * sign, own_f[0:HALF] * -sign], 0)
        x_f = before_f + moved_f
        lg_f = dot3(fh, fl, lg)
        h_f = dot3(fh_half, fl_half, taps)

        long = dot3(long_ref[0], long_ref[1], times(x_f, h_f))
        pg = dot3(grad_ref[0], grad_ref[1], times_conj(lg_f, h_f))
        filt = dot3(grad_ref[0, 0:ROWS], grad_ref[1, 0:ROWS], times_conj(lg_f, own_f))

        h0, h1, h127 = taps[0:1], taps[1:2], taps[127:128]
        p0, p1 = p_far[0:1], p_far[1:2]
        fix_long = jnp.where(row == 0, h0 * p0, jnp.where(row == 1, h0 * p1 + h1 * p0, 0.0))
        fix_grad = jnp.where(row == 1, h127 * lg[0:1], 0.0)
        long_own, long_far = long[0:128], long[128:136] + fix_long
        pg_own, pg_far = pg[0:128], pg[128:136] + fix_grad

        mixed = a0[0:128] * long_own
        mixed_ref[:, cols] = mixed.astype(BF16)

        def finish(s, err_own, err_far, ext, base, out_ref):
            e_ext[0:128] = err_own
            e_ext[128:136] = err_far
            total = tap(s, 0) * err_own + tap(s, 1) * e_ext[1:129] + tap(s, 2) * e_ext[2:130]
            out_ref[:, cols] = total.astype(BF16)
            for j in range(3):
                short_all[3 * s + j : 3 * s + j + 1, cols] = jnp.sum(
                    err_own * ext[base - j : base - j + 128], axis=0, keepdims=True
                )
            return total

        gq = finish(0, cot * long_own, cot_next[0:8] * long_far, q_ext, 8, gq_ref)
        gk = finish(1, pg_own * a2[128:256], pg_far * a2[256:264], k_ext, 136, gk_ref)
        gv = finish(2, pg_own * a1[128:256], pg_far * a1[256:264], v_ext, 136, gv_ref)
        lacking = cot_next[0:1] * h127 * p_own[1:2]
        for j in range(3):
            short_all[j : j + 1, cols] += lacking * q_ext[136 - j : 137 - j]

        late_ref[0, :, cols] = p_own[1:2]
        late_ref[1, :, cols] = lg[128:129]
        fix_ref[0:1, cols] = mixed[0:1]
        fix_ref[1:2, cols] = gq[0:1]
        fix_ref[2:3, cols] = gk[127:128]
        fix_ref[3:4, cols] = gv[127:128]
        fix_ref[4:5, cols] = a0[0:1] * h127
        fix_ref[5:6, cols] = tap(0, 0) * cot[0:1] * h127
        fix_ref[6:7, cols] = tap(1, 2) * h127 * a2[257:258]
        fix_ref[7:8, cols] = tap(2, 2) * h127 * a1[257:258]

        for part in range(WIDE // TILE):
            h = step * (WIDE // TILE) + part
            lanes = slice(part * TILE, (part + 1) * TILE)
            for g in range(16):
                tile = filt[8 * g : 8 * g + 8, lanes]
                part_ref[16 * h + g, 0:8] = tile.reshape(8, 1, TILE)
                if g < 9:
                    value = short_all[g : g + 1, h * TILE : (h + 1) * TILE]
                else:
                    value = jnp.zeros((1, TILE), F32)
                part_ref[16 * h + g, 8] = value


def run_layer(streams, before, after, taps, shorts, matrices):
    channels = streams[0].shape[1]
    out_rows = jax.ShapeDtypeStruct((ROWS, channels), BF16)
    ext = pltpu.VMEM((272, WIDE), F32)
    vmem = pl.BlockSpec(memory_space=pltpu.VMEM)
    return pl.pallas_call(
        layer_kernel,
        in_specs=[vmem] * 11,
        out_specs=[vmem] * 7,
        out_shape=[out_rows] * 4
        + [
            jax.ShapeDtypeStruct((64, CHUNK, 1, TILE), F32),
            jax.ShapeDtypeStruct((8, channels), F32),
            jax.ShapeDtypeStruct((2, 1, channels), F32),
        ],
        scratch_shapes=[
            ext, ext, ext,
            pltpu.VMEM((OUT, WIDE), F32),
            pltpu.VMEM((16, channels), F32),
        ],
        compiler_params=pltpu.CompilerParams(vmem_limit_bytes=VMEM_LIMIT),
        name="layer",
    )(*streams, before, after, taps, shorts, *matrices)


def sum_kernel(part_ref, tile_ref, short_ref):
    total = jnp.sum(part_ref[...], axis=0)
    tile_ref[...] = total[0:8]
    short_ref[...] = total[8:9]


def patch_kernel(
    p_ref, lg_ref, fix_ref, mixed_in, gq_in, gk_in, gv_in, mixed_ref, gq_ref, gk_ref, gv_ref
):
    row = lax.broadcasted_iota(jnp.int32, (EDGE, p_ref.shape[2]), 0)
    plan = (
        (0, p_ref, 0, mixed_in, mixed_ref),
        (1, p_ref, 0, gq_in, gq_ref),
        (2, lg_ref, EDGE - 1, gk_in, gk_ref),
        (3, lg_ref, EDGE - 1, gv_in, gv_ref),
    )
    for n, late_ref, place, old_ref, new_ref in plan:
        value = fix_ref[n : n + 1] + fix_ref[4 + n : 5 + n] * late_ref[0]
        old = old_ref[...].astype(F32)
        new_ref[...] = jnp.where(row == place, value, old).astype(BF16)


def patch(late_p, late_lg, fix, outs):
    channels = outs[0].shape[1]

    def edge(block):
        return pl.BlockSpec((EDGE, channels), lambda i: (block, 0))

    edges = [edge(0), edge(0), edge(ROWS // EDGE - 1), edge(ROWS // EDGE - 1)]
    return pl.pallas_call(
        patch_kernel,
        grid=(1,),
        in_specs=[
            pl.BlockSpec(late_p.shape, lambda i: (0, 0, 0)),
            pl.BlockSpec(late_lg.shape, lambda i: (0, 0, 0)),
            pl.BlockSpec(fix.shape, lambda i: (0, 0)),
        ]
        + edges,
        out_specs=edges,
        out_shape=[jax.ShapeDtypeStruct(o.shape, o.dtype) for o in outs],
        input_output_aliases={3: 0, 4: 1, 5: 2, 6: 3},
        compiler_params=SMALL,
        name="patch",
    )(late_p, late_lg, fix, *outs)


def spread_kernel(tile_ref, short_ref, late_ref, out_ref, p_ref, lg_ref):
    peers = out_ref.shape[0]
    out_ref[:, 0:8] = jnp.broadcast_to(tile_ref[...][None], (peers, 8, 1, TILE))
    out_ref[:, 8:9] = jnp.broadcast_to(short_ref[...][None], (peers, 1, 1, TILE))
    p_ref[...] = late_ref[0:1]
    lg_ref[...] = late_ref[1:2]


def final_kernel(scale, groups, gathered_ref, filter_ref, short_ref):
    for h in range(4):
        for d in range(groups):
            for half in range(2):
                tile = gathered_ref[h * 16 + d * 2 + half, 0:8].reshape(8, TILE)
                start = (d * 4 + h) * TILE
                filter_ref[8 * half : 8 * half + 8, start : start + TILE] = tile * scale
        for g in range(9):
            row = gathered_ref[h * 16 + g, 8] * scale
            short_ref[g : g + 1, h * TILE : (h + 1) * TILE] = row


def on_device(q_stream, k_stream, v_stream, filter_taps, short_taps, cotangent, *, matrices):
    groups, peers = lax.axis_size("dp"), lax.axis_size("ctx")

    def shifted(value, by):
        pairs = [(i, i + by) for i in range(peers) if 0 <= i + by < peers]
        return lax.ppermute(value, "ctx", pairs)

    right, left = pack(q_stream, k_stream, v_stream, cotangent)
    before = shifted(right, 1)
    after = shifted(left, -1)
    taps = lax.all_to_all(filter_taps, "dp", split_axis=1, concat_axis=0, tiled=True)

    *outs, part, fix, late = run_layer(
        (q_stream, k_stream, v_stream, cotangent),
        before,
        after,
        taps,
        short_taps,
        matrices,
    )

    part = lax.all_to_all(part, "ctx", split_axis=0, concat_axis=0, tiled=True)
    vmem = pl.BlockSpec(memory_space=pltpu.VMEM)
    tile, short = pl.pallas_call(
        sum_kernel,
        in_specs=[vmem],
        out_specs=[vmem] * 2,
        out_shape=[
            jax.ShapeDtypeStruct((8, 1, TILE), F32),
            jax.ShapeDtypeStruct((1, 1, TILE), F32),
        ],
        compiler_params=SMALL,
        name="sum",
    )(part)

    pairs = [
        (d * peers + h * 16 + e * 2 + half, e * peers + h * 16 + d * 2 + half)
        for d in range(groups)
        for h in range(4)
        for e in range(groups)
        for half in range(2)
    ]
    tile = lax.ppermute(tile, ("dp", "ctx"), pairs)
    edge_row = jax.ShapeDtypeStruct((1, 1, q_stream.shape[1]), F32)
    sent, late_p, late_lg = pl.pallas_call(
        spread_kernel,
        out_shape=[jax.ShapeDtypeStruct((peers, CHUNK, 1, TILE), F32), edge_row, edge_row],
        compiler_params=SMALL,
        name="spread",
    )(tile, short, late)
    outs = patch(shifted(late_p, 1), shifted(late_lg, -1), fix, outs)
    gathered = lax.all_to_all(sent, "ctx", split_axis=0, concat_axis=0, tiled=True)
    scale = 1.0 / math.sqrt(ROWS * peers)
    grad_filter, grad_short = pl.pallas_call(
        functools.partial(final_kernel, scale, groups),
        out_shape=[
            jax.ShapeDtypeStruct(filter_taps.shape, F32),
            jax.ShapeDtypeStruct(short_taps.shape, F32),
        ],
        compiler_params=SMALL,
        name="final",
    )(gathered)
    return (*outs, grad_filter, grad_short)


def solution(mesh):
    streams = P("ctx", "dp")
    in_specs = (streams, streams, streams, P("dp", None), P(None, "dp"), streams)
    out_specs = (streams,) * 4 + (P("dp", None), P(None, "dp"))
    matrices = transform_matrices()
    return jax.shard_map(
        functools.partial(on_device, matrices=matrices),
        mesh=mesh,
        in_specs=in_specs,
        out_specs=out_specs,
        check_vma=False,
    )
```

```python
import functools
import math

import jax
import jax.numpy as jnp
import ml_dtypes
import numpy as np
from jax import lax
from jax.experimental import pallas as pl
from jax.experimental.pallas import tpu as pltpu
from jax.sharding import PartitionSpec as P

BF16 = jnp.bfloat16
F32 = jnp.float32

ROWS = 128
PERIOD = 256
HALF = PERIOD // 2
OUT = 136
WIDE = 256
EDGE = 16
TILE = 128
FAR_ROWS = 288
CHUNK = 9
VMEM_LIMIT = 24 * 1024 * 1024
SMALL = pltpu.CompilerParams(vmem_limit_bytes=8 * 1024 * 1024)


def two_parts(matrix):
    high = matrix.astype(ml_dtypes.bfloat16)
    low = (matrix - high.astype(np.float64)).astype(ml_dtypes.bfloat16)
    return np.stack([high, low])


def transform_matrices():
    freqs = np.arange(HALF) + 0.5

    def angles(places):
        return 2.0 * np.pi * np.outer(freqs, places) / PERIOD

    forward = angles(np.arange(PERIOD))
    forward = np.concatenate([np.cos(forward), -np.sin(forward)], 0)

    def inverse(places):
        turned = angles(places).T
        return np.concatenate([np.cos(turned), -np.sin(turned)], 1) * (2.0 / PERIOD)

    long_back = inverse(np.arange(HALF, HALF + OUT))
    grad_back = inverse(np.arange(OUT))
    return tuple(two_parts(m) for m in (forward, long_back, grad_back))


def split(value):
    high = value.astype(BF16)
    low = (value - high.astype(F32)).astype(BF16)
    return high, low


def dot3(matrix_high, matrix_low, value):
    high, low = split(value)
    dot = functools.partial(jnp.dot, preferred_element_type=F32)
    return dot(matrix_high, high) + (dot(matrix_high, low) + dot(matrix_low, high))


def pack_kernel(place_ref, q_ref, k_ref, v_ref, c_ref, far_ref, near_ref):
    def to_right(ref):
        ref[0:ROWS] = k_ref[...]
        ref[ROWS : 2 * ROWS] = v_ref[...]
        ref[2 * ROWS : 2 * ROWS + EDGE] = q_ref[ROWS - EDGE : ROWS]

    def to_left(ref):
        ref[0:ROWS] = q_ref[...]
        ref[ROWS : 2 * ROWS] = c_ref[...]
        ref[2 * ROWS : 2 * ROWS + EDGE] = k_ref[0:EDGE]
        ref[2 * ROWS + EDGE : 2 * ROWS + 2 * EDGE] = v_ref[0:EDGE]

    odd = lax.rem(place_ref[0], 2) == 1

    @pl.when(odd)
    def _():
        to_right(far_ref)
        to_left(near_ref)

    @pl.when(jnp.logical_not(odd))
    def _():
        to_left(far_ref)
        to_right(near_ref)


def pack(place, q_stream, k_stream, v_stream, cotangent):
    channels = q_stream.shape[1]
    vmem = pl.BlockSpec(memory_space=pltpu.VMEM)
    return pl.pallas_call(
        pack_kernel,
        in_specs=[pl.BlockSpec(memory_space=pltpu.SMEM)] + [vmem] * 4,
        out_specs=[vmem] * 2,
        out_shape=[
            jax.ShapeDtypeStruct((FAR_ROWS, channels), BF16),
            jax.ShapeDtypeStruct((2 * ROWS + 2 * EDGE, channels), BF16),
        ],
        compiler_params=SMALL,
        name="pack",
    )(place, q_stream, k_stream, v_stream, cotangent)


def seat(h, owner, half):
    return 16 * h + 8 * half + 2 * (owner % 4) + owner // 4


def layer_kernel(
    place_ref,
    q_ref, k_ref, v_ref, c_ref, far_ref, near_ref,
    h_ref, s_ref, fwd_ref, long_ref, grad_ref,
    mixed_ref, gq_ref, gk_ref, gv_ref, part_ref, fix_ref, late_ref,
    q_ext, k_ext, v_ext, c_next, e_ext, short_all,
):
    def f32(x):
        return x.astype(F32)

    odd = lax.rem(place_ref[0], 2) == 1
    fh, fl = fwd_ref[0], fwd_ref[1]
    fh_half, fl_half = fh[:, 0:HALF], fl[:, 0:HALF]
    freq = lax.broadcasted_iota(jnp.int32, (HALF, WIDE), 0)
    sign = jnp.where(freq % 2 == 0, 1.0, -1.0).astype(F32)
    row = lax.broadcasted_iota(jnp.int32, (8, WIDE), 0)

    def times(a, b):
        ar, ai, br, bi = a[0:HALF], a[HALF:], b[0:HALF], b[HALF:]
        return jnp.concatenate([ar * br - ai * bi, ar * bi + ai * br], 0)

    def times_conj(a, b):
        ar, ai, br, bi = a[0:HALF], a[HALF:], b[0:HALF], b[HALF:]
        return jnp.concatenate([ar * br + ai * bi, ai * br - ar * bi], 0)

    for step in range(q_ref.shape[1] // WIDE):
        cols = pl.ds(step * WIDE, WIDE)

        def stage(before_ref, after_ref):
            q_ext[0:8] = f32(before_ref[2 * ROWS : 2 * ROWS + EDGE, cols])[8:16]
            q_ext[136:264] = f32(after_ref[0:ROWS, cols])
            c_next[...] = f32(after_ref[ROWS : 2 * ROWS, cols])
            for n, ext in ((0, k_ext), (1, v_ext)):
                ext[8:136] = f32(before_ref[ROWS * n : ROWS * (n + 1), cols])
                start = 2 * ROWS + EDGE * n
                ext[264:272] = f32(after_ref[start : start + EDGE, cols])[0:8]

        @pl.when(odd)
        def _():
            stage(near_ref, far_ref)

        @pl.when(jnp.logical_not(odd))
        def _():
            stage(far_ref, near_ref)

        q_ext[8:136] = f32(q_ref[:, cols])
        for ext, own in ((k_ext, k_ref), (v_ext, v_ref)):
            ext[0:8] = jnp.zeros((8, WIDE), F32)
            ext[136:264] = f32(own[:, cols])

        def tap(s, j):
            return s_ref[3 * s + j : 3 * s + j + 1, cols]

        def causal(ext, s, count):
            return (
                tap(s, 0) * ext[8 : 8 + count]
                + tap(s, 1) * ext[7 : 7 + count]
                + tap(s, 2) * ext[6 : 6 + count]
            )

        a0 = causal(q_ext, 0, 256)
        a1 = causal(k_ext, 1, 264)
        a2 = causal(v_ext, 2, 264)
        product = a1 * a2
        p_before = jnp.concatenate([jnp.where(row < 2, 0.0, product[0:8]), product[8:128]], 0)
        p_own, p_far = product[128:256], product[256:264]
        cot = f32(c_ref[:, cols])
        cot_next = c_next[...]
        lg = jnp.concatenate([cot, cot_next], 0) * a0

        taps = h_ref[:, cols]
        own_f = dot3(fh_half, fl_half, p_own)
        before_f = dot3(fh_half, fl_half, p_before)
        moved_f = jnp.concatenate([own_f[HALF:] * sign, own_f[0:HALF] * -sign], 0)
        x_f = before_f + moved_f
        lg_f = dot3(fh, fl, lg)
        h_f = dot3(fh_half, fl_half, taps)

        long = dot3(long_ref[0], long_ref[1], times(x_f, h_f))
        pg = dot3(grad_ref[0], grad_ref[1], times_conj(lg_f, h_f))
        filt = dot3(grad_ref[0, 0:ROWS], grad_ref[1, 0:ROWS], times_conj(lg_f, own_f))

        h0, h1, h127 = taps[0:1], taps[1:2], taps[127:128]
        p0, p1 = p_far[0:1], p_far[1:2]
        fix_long = jnp.where(row == 0, h0 * p0, jnp.where(row == 1, h0 * p1 + h1 * p0, 0.0))
        fix_grad = jnp.where(row == 1, h127 * lg[0:1], 0.0)
        long_own, long_far = long[0:128], long[128:136] + fix_long
        pg_own, pg_far = pg[0:128], pg[128:136] + fix_grad

        mixed = a0[0:128] * long_own
        mixed_ref[:, cols] = mixed.astype(BF16)

        def finish(s, err_own, err_far, ext, base, out_ref):
            e_ext[0:128] = err_own
            e_ext[128:136] = err_far
            total = tap(s, 0) * err_own + tap(s, 1) * e_ext[1:129] + tap(s, 2) * e_ext[2:130]
            out_ref[:, cols] = total.astype(BF16)
            for j in range(3):
                short_all[3 * s + j : 3 * s + j + 1, cols] = jnp.sum(
                    err_own * ext[base - j : base - j + 128], axis=0, keepdims=True
                )
            return total

        gq = finish(0, cot * long_own, cot_next[0:8] * long_far, q_ext, 8, gq_ref)
        gk = finish(1, pg_own * a2[128:256], pg_far * a2[256:264], k_ext, 136, gk_ref)
        gv = finish(2, pg_own * a1[128:256], pg_far * a1[256:264], v_ext, 136, gv_ref)
        lacking = cot_next[0:1] * h127 * p_own[1:2]
        for j in range(3):
            short_all[j : j + 1, cols] += lacking * q_ext[136 - j : 137 - j]

        late_ref[0, :, cols] = p_own[1:2]
        late_ref[1, :, cols] = lg[128:129]
        fix_ref[0:1, cols] = mixed[0:1]
        fix_ref[1:2, cols] = gq[0:1]
        fix_ref[2:3, cols] = gk[127:128]
        fix_ref[3:4, cols] = gv[127:128]
        fix_ref[4:5, cols] = a0[0:1] * h127
        fix_ref[5:6, cols] = tap(0, 0) * cot[0:1] * h127
        fix_ref[6:7, cols] = tap(1, 2) * h127 * a2[257:258]
        fix_ref[7:8, cols] = tap(2, 2) * h127 * a1[257:258]

        for part in range(WIDE // TILE):
            h = step * (WIDE // TILE) + part
            lanes = slice(part * TILE, (part + 1) * TILE)
            for g in range(16):
                tile = filt[8 * g : 8 * g + 8, lanes]
                part_ref[seat(h, g // 2, g % 2), 0:8] = tile.reshape(8, 1, TILE)
                if g < 9:
                    value = short_all[g : g + 1, h * TILE : (h + 1) * TILE]
                else:
                    value = jnp.zeros((1, TILE), F32)
                part_ref[seat(h, g // 2, g % 2), 8] = value


def run_layer(place, streams, far, near, taps, shorts, matrices):
    channels = streams[0].shape[1]
    out_rows = jax.ShapeDtypeStruct((ROWS, channels), BF16)
    ext = pltpu.VMEM((272, WIDE), F32)
    vmem = pl.BlockSpec(memory_space=pltpu.VMEM)
    return pl.pallas_call(
        layer_kernel,
        in_specs=[pl.BlockSpec(memory_space=pltpu.SMEM)] + [vmem] * 11,
        out_specs=[vmem] * 7,
        out_shape=[out_rows] * 4
        + [
            jax.ShapeDtypeStruct((64, CHUNK, 1, TILE), F32),
            jax.ShapeDtypeStruct((8, channels), F32),
            jax.ShapeDtypeStruct((2, 1, channels), F32),
        ],
        scratch_shapes=[
            ext, ext, ext,
            pltpu.VMEM((ROWS, WIDE), F32),
            pltpu.VMEM((OUT, WIDE), F32),
            pltpu.VMEM((16, channels), F32),
        ],
        compiler_params=pltpu.CompilerParams(vmem_limit_bytes=VMEM_LIMIT),
        name="layer",
    )(place, *streams, far, near, taps, shorts, *matrices)


def sum_kernel(part_ref, tile_ref, short_ref):
    total = jnp.sum(part_ref[...], axis=0)
    tile_ref[...] = total[0:8]
    short_ref[...] = total[8:9]


def patch_kernel(
    p_ref, lg_ref, fix_ref, mixed_in, gq_in, gk_in, gv_in, mixed_ref, gq_ref, gk_ref, gv_ref
):
    row = lax.broadcasted_iota(jnp.int32, (EDGE, p_ref.shape[2]), 0)
    plan = (
        (0, p_ref, 0, 0, mixed_in, mixed_ref),
        (1, p_ref, 0, 0, gq_in, gq_ref),
        (2, lg_ref, ROWS - EDGE, EDGE - 1, gk_in, gk_ref),
        (3, lg_ref, ROWS - EDGE, EDGE - 1, gv_in, gv_ref),
    )
    for n, late_ref, start, place, old_ref, new_ref in plan:
        new_ref[...] = old_ref[...]
        value = fix_ref[n : n + 1] + fix_ref[4 + n : 5 + n] * late_ref[0]
        old = old_ref[start : start + EDGE].astype(F32)
        new_ref[start : start + EDGE] = jnp.where(row == place, value, old).astype(BF16)


def patch(late_p, late_lg, fix, outs):
    vmem = pl.BlockSpec(memory_space=pltpu.VMEM)
    return pl.pallas_call(
        patch_kernel,
        in_specs=[vmem] * 7,
        out_specs=[vmem] * 4,
        out_shape=[jax.ShapeDtypeStruct(o.shape, o.dtype) for o in outs],
        compiler_params=SMALL,
        name="patch",
    )(late_p, late_lg, fix, *outs)


def spread_kernel(tile_ref, short_ref, late_ref, out_ref, p_ref, lg_ref):
    peers = out_ref.shape[0]
    out_ref[:, 0:8] = jnp.broadcast_to(tile_ref[...][None], (peers, 8, 1, TILE))
    out_ref[:, 8:9] = jnp.broadcast_to(short_ref[...][None], (peers, 1, 1, TILE))
    p_ref[...] = late_ref[0:1]
    lg_ref[...] = late_ref[1:2]


def final_kernel(scale, groups, gathered_ref, filter_ref, short_ref):
    for h in range(4):
        for d in range(groups):
            for half in range(2):
                tile = gathered_ref[seat(h, d, half), 0:8].reshape(8, TILE)
                start = (d * 4 + h) * TILE
                filter_ref[8 * half : 8 * half + 8, start : start + TILE] = tile * scale
        for g in range(9):
            row = gathered_ref[seat(h, g // 2, g % 2), 8] * scale
            short_ref[g : g + 1, h * TILE : (h + 1) * TILE] = row


def on_device(q_stream, k_stream, v_stream, filter_taps, short_taps, cotangent, *, matrices):
    groups, peers = lax.axis_size("dp"), lax.axis_size("ctx")

    def shifted(value, by):
        pairs = [(i, i + by) for i in range(peers) if 0 <= i + by < peers]
        return lax.ppermute(value, "ctx", pairs)

    place = lax.axis_index("ctx").astype(jnp.int32).reshape(1)
    far, near = pack(place, q_stream, k_stream, v_stream, cotangent)
    far = lax.ppermute(
        far, "ctx", [(i, i + 1 if i % 2 else i - 1) for i in range(1, peers - 1)]
    )
    near = lax.ppermute(near, "ctx", [(i, i ^ 1) for i in range(peers)])
    taps = lax.all_to_all(filter_taps, "dp", split_axis=1, concat_axis=0, tiled=True)

    *outs, part, fix, late = run_layer(
        place,
        (q_stream, k_stream, v_stream, cotangent),
        far,
        near,
        taps,
        short_taps,
        matrices,
    )

    part = lax.all_to_all(part, "ctx", split_axis=0, concat_axis=0, tiled=True)
    vmem = pl.BlockSpec(memory_space=pltpu.VMEM)
    tile, short = pl.pallas_call(
        sum_kernel,
        in_specs=[vmem],
        out_specs=[vmem] * 2,
        out_shape=[
            jax.ShapeDtypeStruct((8, 1, TILE), F32),
            jax.ShapeDtypeStruct((1, 1, TILE), F32),
        ],
        compiler_params=SMALL,
        name="sum",
    )(part)

    pairs = [
        (d * peers + seat(h, e, half), e * peers + seat(h, d, half))
        for d in range(groups)
        for h in range(4)
        for e in range(groups)
        for half in range(2)
    ]
    tile = lax.ppermute(tile, ("dp", "ctx"), pairs)
    edge_row = jax.ShapeDtypeStruct((1, 1, q_stream.shape[1]), F32)
    sent, late_p, late_lg = pl.pallas_call(
        spread_kernel,
        out_shape=[jax.ShapeDtypeStruct((peers, CHUNK, 1, TILE), F32), edge_row, edge_row],
        compiler_params=SMALL,
        name="spread",
    )(tile, short, late)
    outs = patch(shifted(late_p, 1), shifted(late_lg, -1), fix, outs)
    gathered = lax.all_to_all(sent, "ctx", split_axis=0, concat_axis=0, tiled=True)
    scale = 1.0 / math.sqrt(ROWS * peers)
    grad_filter, grad_short = pl.pallas_call(
        functools.partial(final_kernel, scale, groups),
        out_shape=[
            jax.ShapeDtypeStruct(filter_taps.shape, F32),
            jax.ShapeDtypeStruct(short_taps.shape, F32),
        ],
        compiler_params=SMALL,
        name="final",
    )(gathered)
    return (*outs, grad_filter, grad_short)


def solution(mesh):
    streams = P("ctx", "dp")
    in_specs = (streams, streams, streams, P("dp", None), P(None, "dp"), streams)
    out_specs = (streams,) * 4 + (P("dp", None), P(None, "dp"))
    matrices = transform_matrices()
    return jax.shard_map(
        functools.partial(on_device, matrices=matrices),
        mesh=mesh,
        in_specs=in_specs,
        out_specs=out_specs,
        check_vma=False,
    )
```

```python
import functools
import math

import jax
import jax.numpy as jnp
import ml_dtypes
import numpy as np
from jax import lax
from jax.experimental import pallas as pl
from jax.experimental.pallas import tpu as pltpu
from jax.sharding import PartitionSpec as P

BF16 = jnp.bfloat16
F32 = jnp.float32

ROWS = 128
PERIOD = 256
HALF = PERIOD // 2
OUT = 136
WIDE = 256
EDGE = 16
TILE = 128
FAR_ROWS = 288
CHUNK = 9
VMEM_LIMIT = 24 * 1024 * 1024
SMALL = pltpu.CompilerParams(vmem_limit_bytes=8 * 1024 * 1024)


def two_parts(matrix):
    high = matrix.astype(ml_dtypes.bfloat16)
    low = (matrix - high.astype(np.float64)).astype(ml_dtypes.bfloat16)
    return np.concatenate([high, low, high], 1)


def transform_matrices():
    freqs = np.arange(HALF) + 0.5

    def angles(places):
        return 2.0 * np.pi * np.outer(freqs, places) / PERIOD

    forward = angles(np.arange(PERIOD))
    forward = np.concatenate([np.cos(forward), -np.sin(forward)], 0)

    def inverse(places):
        turned = angles(places).T
        return np.concatenate([np.cos(turned), -np.sin(turned)], 1) * (2.0 / PERIOD)

    long_back = inverse(np.arange(HALF, HALF + OUT))
    grad_back = inverse(np.arange(OUT))
    return tuple(two_parts(m) for m in (forward, long_back, grad_back))


def split(value):
    high = value.astype(BF16)
    low = (value - high.astype(F32)).astype(BF16)
    return high, low


def dot3(matrix, value):
    high, low = split(value)
    parts = jnp.concatenate([high, high, low], 0)
    return jnp.dot(matrix, parts, preferred_element_type=F32)


def pack_kernel(place_ref, q_ref, k_ref, v_ref, c_ref, far_ref, near_ref):
    def to_right(ref):
        ref[0:ROWS] = k_ref[...]
        ref[ROWS : 2 * ROWS] = v_ref[...]
        ref[2 * ROWS : 2 * ROWS + EDGE] = q_ref[ROWS - EDGE : ROWS]

    def to_left(ref):
        ref[0:ROWS] = q_ref[...]
        ref[ROWS : 2 * ROWS] = c_ref[...]
        ref[2 * ROWS : 2 * ROWS + EDGE] = k_ref[0:EDGE]
        ref[2 * ROWS + EDGE : 2 * ROWS + 2 * EDGE] = v_ref[0:EDGE]

    odd = lax.rem(place_ref[0], 2) == 1

    @pl.when(odd)
    def _():
        to_right(far_ref)
        to_left(near_ref)

    @pl.when(jnp.logical_not(odd))
    def _():
        to_left(far_ref)
        to_right(near_ref)


def pack(place, q_stream, k_stream, v_stream, cotangent):
    channels = q_stream.shape[1]
    vmem = pl.BlockSpec(memory_space=pltpu.VMEM)
    return pl.pallas_call(
        pack_kernel,
        in_specs=[pl.BlockSpec(memory_space=pltpu.SMEM)] + [vmem] * 4,
        out_specs=[vmem] * 2,
        out_shape=[
            jax.ShapeDtypeStruct((FAR_ROWS, channels), BF16),
            jax.ShapeDtypeStruct((2 * ROWS + 2 * EDGE, channels), BF16),
        ],
        compiler_params=SMALL,
        name="pack",
    )(place, q_stream, k_stream, v_stream, cotangent)


def seat(h, owner, half):
    return 16 * h + 8 * half + 2 * (owner % 4) + owner // 4


def layer_kernel(
    place_ref,
    q_ref, k_ref, v_ref, c_ref, far_ref, near_ref,
    h_ref, s_ref, fwd_ref, long_ref, grad_ref,
    mixed_ref, gq_ref, gk_ref, gv_ref, part_ref, fix_ref, late_ref,
    q_ext, k_ext, v_ext, c_next, e_ext, short_all,
):
    def f32(x):
        return x.astype(F32)

    odd = lax.rem(place_ref[0], 2) == 1
    half = jnp.concatenate([fwd_ref[:, PERIOD * n : PERIOD * n + HALF] for n in range(3)], 1)
    freq = lax.broadcasted_iota(jnp.int32, (HALF, WIDE), 0)
    sign = jnp.where(freq % 2 == 0, 1.0, -1.0).astype(F32)
    row = lax.broadcasted_iota(jnp.int32, (8, WIDE), 0)

    def times(a, b):
        ar, ai, br, bi = a[0:HALF], a[HALF:], b[0:HALF], b[HALF:]
        return jnp.concatenate([ar * br - ai * bi, ar * bi + ai * br], 0)

    def times_conj(a, b):
        ar, ai, br, bi = a[0:HALF], a[HALF:], b[0:HALF], b[HALF:]
        return jnp.concatenate([ar * br + ai * bi, ai * br - ar * bi], 0)

    for step in range(q_ref.shape[1] // WIDE):
        cols = pl.ds(step * WIDE, WIDE)

        def stage(before_ref, after_ref):
            q_ext[0:8] = f32(before_ref[2 * ROWS : 2 * ROWS + EDGE, cols])[8:16]
            q_ext[136:264] = f32(after_ref[0:ROWS, cols])
            c_next[...] = f32(after_ref[ROWS : 2 * ROWS, cols])
            for n, ext in ((0, k_ext), (1, v_ext)):
                ext[8:136] = f32(before_ref[ROWS * n : ROWS * (n + 1), cols])
                start = 2 * ROWS + EDGE * n
                ext[264:272] = f32(after_ref[start : start + EDGE, cols])[0:8]

        @pl.when(odd)
        def _():
            stage(near_ref, far_ref)

        @pl.when(jnp.logical_not(odd))
        def _():
            stage(far_ref, near_ref)

        q_ext[8:136] = f32(q_ref[:, cols])
        for ext, own in ((k_ext, k_ref), (v_ext, v_ref)):
            ext[0:8] = jnp.zeros((8, WIDE), F32)
            ext[136:264] = f32(own[:, cols])

        def tap(s, j):
            return s_ref[3 * s + j : 3 * s + j + 1, cols]

        def causal(ext, s, count):
            return (
                tap(s, 0) * ext[8 : 8 + count]
                + tap(s, 1) * ext[7 : 7 + count]
                + tap(s, 2) * ext[6 : 6 + count]
            )

        a0 = causal(q_ext, 0, 256)
        a1 = causal(k_ext, 1, 264)
        a2 = causal(v_ext, 2, 264)
        product = a1 * a2
        p_before = jnp.concatenate([jnp.where(row < 2, 0.0, product[0:8]), product[8:128]], 0)
        p_own, p_far = product[128:256], product[256:264]
        cot = f32(c_ref[:, cols])
        cot_next = c_next[...]
        lg = jnp.concatenate([cot, cot_next], 0) * a0

        taps = h_ref[:, cols]
        own_f = dot3(half, p_own)
        before_f = dot3(half, p_before)
        moved_f = jnp.concatenate([own_f[HALF:] * sign, own_f[0:HALF] * -sign], 0)
        x_f = before_f + moved_f
        lg_f = dot3(fwd_ref[...], lg)
        h_f = dot3(half, taps)

        long = dot3(long_ref[...], times(x_f, h_f))
        pg = dot3(grad_ref[...], times_conj(lg_f, h_f))
        filt = dot3(grad_ref[0:ROWS], times_conj(lg_f, own_f))

        h0, h1, h127 = taps[0:1], taps[1:2], taps[127:128]
        p0, p1 = p_far[0:1], p_far[1:2]
        fix_long = jnp.where(row == 0, h0 * p0, jnp.where(row == 1, h0 * p1 + h1 * p0, 0.0))
        fix_grad = jnp.where(row == 1, h127 * lg[0:1], 0.0)
        long_own, long_far = long[0:128], long[128:136] + fix_long
        pg_own, pg_far = pg[0:128], pg[128:136] + fix_grad

        mixed = a0[0:128] * long_own
        mixed_ref[:, cols] = mixed.astype(BF16)

        def finish(s, err_own, err_far, ext, base, out_ref):
            e_ext[0:128] = err_own
            e_ext[128:136] = err_far
            total = tap(s, 0) * err_own + tap(s, 1) * e_ext[1:129] + tap(s, 2) * e_ext[2:130]
            out_ref[:, cols] = total.astype(BF16)
            for j in range(3):
                short_all[3 * s + j : 3 * s + j + 1, cols] = jnp.sum(
                    err_own * ext[base - j : base - j + 128], axis=0, keepdims=True
                )
            return total

        gq = finish(0, cot * long_own, cot_next[0:8] * long_far, q_ext, 8, gq_ref)
        gk = finish(1, pg_own * a2[128:256], pg_far * a2[256:264], k_ext, 136, gk_ref)
        gv = finish(2, pg_own * a1[128:256], pg_far * a1[256:264], v_ext, 136, gv_ref)
        lacking = cot_next[0:1] * h127 * p_own[1:2]
        for j in range(3):
            short_all[j : j + 1, cols] += lacking * q_ext[136 - j : 137 - j]

        late_ref[0, :, cols] = p_own[1:2]
        late_ref[1, :, cols] = lg[128:129]
        fix_ref[0:1, cols] = mixed[0:1]
        fix_ref[1:2, cols] = gq[0:1]
        fix_ref[2:3, cols] = gk[127:128]
        fix_ref[3:4, cols] = gv[127:128]
        fix_ref[4:5, cols] = a0[0:1] * h127
        fix_ref[5:6, cols] = tap(0, 0) * cot[0:1] * h127
        fix_ref[6:7, cols] = tap(1, 2) * h127 * a2[257:258]
        fix_ref[7:8, cols] = tap(2, 2) * h127 * a1[257:258]

        for part in range(WIDE // TILE):
            h = step * (WIDE // TILE) + part
            lanes = slice(part * TILE, (part + 1) * TILE)
            for g in range(16):
                tile = filt[8 * g : 8 * g + 8, lanes]
                part_ref[seat(h, g // 2, g % 2), 0:8] = tile.reshape(8, 1, TILE)
                if g < 9:
                    value = short_all[g : g + 1, h * TILE : (h + 1) * TILE]
                else:
                    value = jnp.zeros((1, TILE), F32)
                part_ref[seat(h, g // 2, g % 2), 8] = value


def run_layer(place, streams, far, near, taps, shorts, matrices):
    channels = streams[0].shape[1]
    out_rows = jax.ShapeDtypeStruct((ROWS, channels), BF16)
    ext = pltpu.VMEM((272, WIDE), F32)
    vmem = pl.BlockSpec(memory_space=pltpu.VMEM)
    return pl.pallas_call(
        layer_kernel,
        in_specs=[pl.BlockSpec(memory_space=pltpu.SMEM)] + [vmem] * 11,
        out_specs=[vmem] * 7,
        out_shape=[out_rows] * 4
        + [
            jax.ShapeDtypeStruct((64, CHUNK, 1, TILE), F32),
            jax.ShapeDtypeStruct((8, channels), F32),
            jax.ShapeDtypeStruct((2, 1, channels), F32),
        ],
        scratch_shapes=[
            ext, ext, ext,
            pltpu.VMEM((ROWS, WIDE), F32),
            pltpu.VMEM((OUT, WIDE), F32),
            pltpu.VMEM((16, channels), F32),
        ],
        compiler_params=pltpu.CompilerParams(vmem_limit_bytes=VMEM_LIMIT),
        name="layer",
    )(place, *streams, far, near, taps, shorts, *matrices)


def sum_kernel(part_ref, tile_ref, short_ref):
    total = jnp.sum(part_ref[...], axis=0)
    tile_ref[...] = total[0:8]
    short_ref[...] = total[8:9]


def patch_kernel(
    p_ref, lg_ref, fix_ref, mixed_in, gq_in, gk_in, gv_in, mixed_ref, gq_ref, gk_ref, gv_ref
):
    row = lax.broadcasted_iota(jnp.int32, (EDGE, p_ref.shape[2]), 0)
    plan = (
        (0, p_ref, 0, 0, mixed_in, mixed_ref),
        (1, p_ref, 0, 0, gq_in, gq_ref),
        (2, lg_ref, ROWS - EDGE, EDGE - 1, gk_in, gk_ref),
        (3, lg_ref, ROWS - EDGE, EDGE - 1, gv_in, gv_ref),
    )
    for n, late_ref, start, place, old_ref, new_ref in plan:
        new_ref[...] = old_ref[...]
        value = fix_ref[n : n + 1] + fix_ref[4 + n : 5 + n] * late_ref[0]
        old = old_ref[start : start + EDGE].astype(F32)
        new_ref[start : start + EDGE] = jnp.where(row == place, value, old).astype(BF16)


def patch(late_p, late_lg, fix, outs):
    vmem = pl.BlockSpec(memory_space=pltpu.VMEM)
    return pl.pallas_call(
        patch_kernel,
        in_specs=[vmem] * 7,
        out_specs=[vmem] * 4,
        out_shape=[jax.ShapeDtypeStruct(o.shape, o.dtype) for o in outs],
        compiler_params=SMALL,
        name="patch",
    )(late_p, late_lg, fix, *outs)


def spread_kernel(tile_ref, short_ref, late_ref, out_ref, p_ref, lg_ref):
    peers = out_ref.shape[0]
    out_ref[:, 0:8] = jnp.broadcast_to(tile_ref[...][None], (peers, 8, 1, TILE))
    out_ref[:, 8:9] = jnp.broadcast_to(short_ref[...][None], (peers, 1, 1, TILE))
    p_ref[...] = late_ref[0:1]
    lg_ref[...] = late_ref[1:2]


def final_kernel(scale, groups, gathered_ref, filter_ref, short_ref):
    for h in range(4):
        for d in range(groups):
            for half in range(2):
                tile = gathered_ref[seat(h, d, half), 0:8].reshape(8, TILE)
                start = (d * 4 + h) * TILE
                filter_ref[8 * half : 8 * half + 8, start : start + TILE] = tile * scale
        for g in range(9):
            row = gathered_ref[seat(h, g // 2, g % 2), 8] * scale
            short_ref[g : g + 1, h * TILE : (h + 1) * TILE] = row


def on_device(q_stream, k_stream, v_stream, filter_taps, short_taps, cotangent, *, matrices):
    groups, peers = lax.axis_size("dp"), lax.axis_size("ctx")

    def shifted(value, by):
        pairs = [(i, i + by) for i in range(peers) if 0 <= i + by < peers]
        return lax.ppermute(value, "ctx", pairs)

    place = lax.axis_index("ctx").astype(jnp.int32).reshape(1)
    far, near = pack(place, q_stream, k_stream, v_stream, cotangent)
    far = lax.ppermute(
        far, "ctx", [(i, i + 1 if i % 2 else i - 1) for i in range(1, peers - 1)]
    )
    near = lax.ppermute(near, "ctx", [(i, i ^ 1) for i in range(peers)])
    taps = lax.all_to_all(filter_taps, "dp", split_axis=1, concat_axis=0, tiled=True)

    *outs, part, fix, late = run_layer(
        place,
        (q_stream, k_stream, v_stream, cotangent),
        far,
        near,
        taps,
        short_taps,
        matrices,
    )

    part = lax.all_to_all(part, "ctx", split_axis=0, concat_axis=0, tiled=True)
    vmem = pl.BlockSpec(memory_space=pltpu.VMEM)
    tile, short = pl.pallas_call(
        sum_kernel,
        in_specs=[vmem],
        out_specs=[vmem] * 2,
        out_shape=[
            jax.ShapeDtypeStruct((8, 1, TILE), F32),
            jax.ShapeDtypeStruct((1, 1, TILE), F32),
        ],
        compiler_params=SMALL,
        name="sum",
    )(part)

    pairs = [
        (d * peers + seat(h, e, half), e * peers + seat(h, d, half))
        for d in range(groups)
        for h in range(4)
        for e in range(groups)
        for half in range(2)
    ]
    tile = lax.ppermute(tile, ("dp", "ctx"), pairs)
    edge_row = jax.ShapeDtypeStruct((1, 1, q_stream.shape[1]), F32)
    sent, late_p, late_lg = pl.pallas_call(
        spread_kernel,
        out_shape=[jax.ShapeDtypeStruct((peers, CHUNK, 1, TILE), F32), edge_row, edge_row],
        compiler_params=SMALL,
        name="spread",
    )(tile, short, late)
    outs = patch(shifted(late_p, 1), shifted(late_lg, -1), fix, outs)
    gathered = lax.all_to_all(sent, "ctx", split_axis=0, concat_axis=0, tiled=True)
    scale = 1.0 / math.sqrt(ROWS * peers)
    grad_filter, grad_short = pl.pallas_call(
        functools.partial(final_kernel, scale, groups),
        out_shape=[
            jax.ShapeDtypeStruct(filter_taps.shape, F32),
            jax.ShapeDtypeStruct(short_taps.shape, F32),
        ],
        compiler_params=SMALL,
        name="final",
    )(gathered)
    return (*outs, grad_filter, grad_short)


def solution(mesh):
    streams = P("ctx", "dp")
    in_specs = (streams, streams, streams, P("dp", None), P(None, "dp"), streams)
    out_specs = (streams,) * 4 + (P("dp", None), P(None, "dp"))
    matrices = transform_matrices()
    return jax.shard_map(
        functools.partial(on_device, matrices=matrices),
        mesh=mesh,
        in_specs=in_specs,
        out_specs=out_specs,
        check_vma=False,
    )
```

```python
import functools
import math

import jax
import jax.numpy as jnp
import ml_dtypes
import numpy as np
from jax import lax
from jax.experimental import pallas as pl
from jax.experimental.pallas import tpu as pltpu
from jax.sharding import PartitionSpec as P

BF16 = jnp.bfloat16
F32 = jnp.float32

ROWS = 128
PERIOD = 256
HALF = PERIOD // 2
OUT = 136
WIDE = 256
EDGE = 16
TILE = 128
FAR_ROWS = 288
CHUNK = 9
VMEM_LIMIT = 24 * 1024 * 1024
SMALL = pltpu.CompilerParams(vmem_limit_bytes=8 * 1024 * 1024)


def two_parts(matrix):
    high = matrix.astype(ml_dtypes.bfloat16)
    low = (matrix - high.astype(np.float64)).astype(ml_dtypes.bfloat16)
    return np.concatenate([high, low, high], 1)


def transform_matrices():
    freqs = np.arange(HALF) + 0.5

    def angles(places):
        return 2.0 * np.pi * np.outer(freqs, places) / PERIOD

    forward = angles(np.arange(PERIOD))
    forward = np.concatenate([np.cos(forward), -np.sin(forward)], 0)

    def inverse(places):
        turned = angles(places).T
        return np.concatenate([np.cos(turned), -np.sin(turned)], 1) * (2.0 / PERIOD)

    long_back = inverse(np.arange(HALF, HALF + OUT))
    grad_back = inverse(np.arange(OUT))
    return tuple(two_parts(m) for m in (forward, long_back, grad_back))


def split(value):
    high = value.astype(BF16)
    low = (value - high.astype(F32)).astype(BF16)
    return high, low


def dot3(matrix, value):
    high, low = split(value)
    parts = jnp.concatenate([high, high, low], 0)
    return jnp.dot(matrix, parts, preferred_element_type=F32)


def pack_kernel(place_ref, q_ref, k_ref, v_ref, c_ref, far_ref, near_ref):
    def to_right(ref):
        ref[0:ROWS] = k_ref[...]
        ref[ROWS : 2 * ROWS] = v_ref[...]
        ref[2 * ROWS : 2 * ROWS + EDGE] = q_ref[ROWS - EDGE : ROWS]

    def to_left(ref):
        ref[0:ROWS] = q_ref[...]
        ref[ROWS : 2 * ROWS] = c_ref[...]
        ref[2 * ROWS : 2 * ROWS + EDGE] = k_ref[0:EDGE]
        ref[2 * ROWS + EDGE : 2 * ROWS + 2 * EDGE] = v_ref[0:EDGE]

    odd = lax.rem(place_ref[0], 2) == 1

    @pl.when(odd)
    def _():
        to_right(far_ref)
        to_left(near_ref)

    @pl.when(jnp.logical_not(odd))
    def _():
        to_left(far_ref)
        to_right(near_ref)


def pack(place, q_stream, k_stream, v_stream, cotangent):
    channels = q_stream.shape[1]
    vmem = pl.BlockSpec(memory_space=pltpu.VMEM)
    return pl.pallas_call(
        pack_kernel,
        in_specs=[pl.BlockSpec(memory_space=pltpu.SMEM)] + [vmem] * 4,
        out_specs=[vmem] * 2,
        out_shape=[
            jax.ShapeDtypeStruct((FAR_ROWS, channels), BF16),
            jax.ShapeDtypeStruct((2 * ROWS + 2 * EDGE, channels), BF16),
        ],
        compiler_params=SMALL,
        name="pack",
    )(place, q_stream, k_stream, v_stream, cotangent)


def seat(h, owner, half):
    return 16 * h + 8 * half + 2 * (owner % 4) + owner // 4


def layer_kernel(
    place_ref,
    q_ref, k_ref, v_ref, c_ref, far_ref, near_ref,
    h_ref, s_ref, fwd_ref, long_ref, grad_ref,
    mixed_ref, eq_ref, ek_ref, ev_ref, part_ref, fix_ref, late_ref,
    q_ext, k_ext, v_ext, c_next, short_all,
):
    def f32(x):
        return x.astype(F32)

    odd = lax.rem(place_ref[0], 2) == 1
    half = jnp.concatenate([fwd_ref[:, PERIOD * n : PERIOD * n + HALF] for n in range(3)], 1)
    freq = lax.broadcasted_iota(jnp.int32, (HALF, WIDE), 0)
    sign = jnp.where(freq % 2 == 0, 1.0, -1.0).astype(F32)
    row = lax.broadcasted_iota(jnp.int32, (8, WIDE), 0)

    def times(a, b):
        ar, ai, br, bi = a[0:HALF], a[HALF:], b[0:HALF], b[HALF:]
        return jnp.concatenate([ar * br - ai * bi, ar * bi + ai * br], 0)

    def times_conj(a, b):
        ar, ai, br, bi = a[0:HALF], a[HALF:], b[0:HALF], b[HALF:]
        return jnp.concatenate([ar * br + ai * bi, ai * br - ar * bi], 0)

    for step in range(q_ref.shape[1] // WIDE):
        cols = pl.ds(step * WIDE, WIDE)

        def stage(before_ref, after_ref):
            q_ext[0:8] = f32(before_ref[2 * ROWS : 2 * ROWS + EDGE, cols])[8:16]
            q_ext[136:264] = f32(after_ref[0:ROWS, cols])
            c_next[...] = f32(after_ref[ROWS : 2 * ROWS, cols])
            for n, ext in ((0, k_ext), (1, v_ext)):
                ext[8:136] = f32(before_ref[ROWS * n : ROWS * (n + 1), cols])
                start = 2 * ROWS + EDGE * n
                ext[264:272] = f32(after_ref[start : start + EDGE, cols])[0:8]

        @pl.when(odd)
        def _():
            stage(near_ref, far_ref)

        @pl.when(jnp.logical_not(odd))
        def _():
            stage(far_ref, near_ref)

        q_ext[8:136] = f32(q_ref[:, cols])
        for ext, own in ((k_ext, k_ref), (v_ext, v_ref)):
            ext[0:8] = jnp.zeros((8, WIDE), F32)
            ext[136:264] = f32(own[:, cols])

        def tap(s, j):
            return s_ref[3 * s + j : 3 * s + j + 1, cols]

        def causal(ext, s, count):
            return (
                tap(s, 0) * ext[8 : 8 + count]
                + tap(s, 1) * ext[7 : 7 + count]
                + tap(s, 2) * ext[6 : 6 + count]
            )

        a0 = causal(q_ext, 0, 256)
        a1 = causal(k_ext, 1, 264)
        a2 = causal(v_ext, 2, 264)
        product = a1 * a2
        p_before = jnp.concatenate([jnp.where(row < 2, 0.0, product[0:8]), product[8:128]], 0)
        p_own, p_far = product[128:256], product[256:264]
        cot = f32(c_ref[:, cols])
        cot_next = c_next[...]
        lg = jnp.concatenate([cot, cot_next], 0) * a0

        taps = h_ref[:, cols]
        own_f = dot3(half, p_own)
        before_f = dot3(half, p_before)
        moved_f = jnp.concatenate([own_f[HALF:] * sign, own_f[0:HALF] * -sign], 0)
        x_f = before_f + moved_f
        lg_f = dot3(fwd_ref[...], lg)
        h_f = dot3(half, taps)

        long = dot3(long_ref[...], times(x_f, h_f))
        pg = dot3(grad_ref[...], times_conj(lg_f, h_f))
        filt = dot3(grad_ref[0:ROWS], times_conj(lg_f, own_f))

        h0, h1, h127 = taps[0:1], taps[1:2], taps[127:128]
        p0, p1 = p_far[0:1], p_far[1:2]
        fix_long = jnp.where(row == 0, h0 * p0, jnp.where(row == 1, h0 * p1 + h1 * p0, 0.0))
        fix_grad = jnp.where(row == 1, h127 * lg[0:1], 0.0)
        long_own, long_far = long[0:128], long[128:136] + fix_long
        pg_own, pg_far = pg[0:128], pg[128:136] + fix_grad

        mixed = a0[0:128] * long_own
        mixed_ref[:, cols] = mixed.astype(BF16)

        def finish(s, err_own, err_far, ext, base, err_ref):
            err_ref[0:128, cols] = err_own
            err_ref[128:136, cols] = err_far
            for j in range(3):
                short_all[3 * s + j : 3 * s + j + 1, cols] = jnp.sum(
                    err_own * ext[base - j : base - j + 128], axis=0, keepdims=True
                )

        finish(0, cot * long_own, cot_next[0:8] * long_far, q_ext, 8, eq_ref)
        finish(1, pg_own * a2[128:256], pg_far * a2[256:264], k_ext, 136, ek_ref)
        finish(2, pg_own * a1[128:256], pg_far * a1[256:264], v_ext, 136, ev_ref)
        lacking = cot_next[0:1] * h127 * p_own[1:2]
        for j in range(3):
            short_all[j : j + 1, cols] += lacking * q_ext[136 - j : 137 - j]

        late_ref[0, :, cols] = p_own[1:2]
        late_ref[1, :, cols] = lg[128:129]
        fix_ref[0:1, cols] = mixed[0:1]
        fix_ref[1:4, cols] = jnp.zeros((3, WIDE), F32)
        fix_ref[4:5, cols] = a0[0:1] * h127
        fix_ref[5:6, cols] = tap(0, 0) * cot[0:1] * h127
        fix_ref[6:7, cols] = tap(1, 2) * h127 * a2[257:258]
        fix_ref[7:8, cols] = tap(2, 2) * h127 * a1[257:258]

        for part in range(WIDE // TILE):
            h = step * (WIDE // TILE) + part
            lanes = slice(part * TILE, (part + 1) * TILE)
            for g in range(16):
                tile = filt[8 * g : 8 * g + 8, lanes]
                part_ref[seat(h, g // 2, g % 2), 0:8] = tile.reshape(8, 1, TILE)
                if g < 9:
                    value = short_all[g : g + 1, h * TILE : (h + 1) * TILE]
                else:
                    value = jnp.zeros((1, TILE), F32)
                part_ref[seat(h, g // 2, g % 2), 8] = value


def run_layer(place, streams, far, near, taps, shorts, matrices):
    channels = streams[0].shape[1]
    out_rows = jax.ShapeDtypeStruct((ROWS, channels), BF16)
    ext = pltpu.VMEM((272, WIDE), F32)
    vmem = pl.BlockSpec(memory_space=pltpu.VMEM)
    return pl.pallas_call(
        layer_kernel,
        in_specs=[pl.BlockSpec(memory_space=pltpu.SMEM)] + [vmem] * 11,
        out_specs=[vmem] * 7,
        out_shape=[out_rows]
        + [jax.ShapeDtypeStruct((OUT, channels), F32)] * 3
        + [
            jax.ShapeDtypeStruct((64, CHUNK, 1, TILE), F32),
            jax.ShapeDtypeStruct((8, channels), F32),
            jax.ShapeDtypeStruct((2, 1, channels), F32),
        ],
        scratch_shapes=[
            ext, ext, ext,
            pltpu.VMEM((ROWS, WIDE), F32),
            pltpu.VMEM((16, channels), F32),
        ],
        compiler_params=pltpu.CompilerParams(vmem_limit_bytes=VMEM_LIMIT),
        name="layer",
    )(place, *streams, far, near, taps, shorts, *matrices)


def sum_kernel(part_ref, tile_ref, short_ref):
    total = jnp.sum(part_ref[...], axis=0)
    tile_ref[...] = total[0:8]
    short_ref[...] = total[8:9]


def patch_kernel(
    p_ref, lg_ref, fix_ref, s_ref, mixed_in, eq_ref, ek_ref, ev_ref,
    mixed_ref, gq_ref, gk_ref, gv_ref,
):
    channels = p_ref.shape[2]
    row = lax.broadcasted_iota(jnp.int32, (EDGE, channels), 0)
    mixed_ref[...] = mixed_in[...]
    value = fix_ref[0:1] + fix_ref[4:5] * p_ref[0]
    old = mixed_in[0:EDGE].astype(F32)
    mixed_ref[0:EDGE] = jnp.where(row == 0, value, old).astype(BF16)
    for s, err_ref, late_ref, place, out_ref in (
        (0, eq_ref, p_ref, 0, gq_ref),
        (1, ek_ref, lg_ref, ROWS - 1, gk_ref),
        (2, ev_ref, lg_ref, ROWS - 1, gv_ref),
    ):
        late = fix_ref[5 + s : 6 + s] * late_ref[0]
        for start in range(0, ROWS, EDGE):
            total = s_ref[3 * s : 3 * s + 1] * err_ref[start : start + EDGE]
            for j in (1, 2):
                total += s_ref[3 * s + j : 3 * s + j + 1] * err_ref[start + j : start + j + EDGE]
            if start <= place < start + EDGE:
                total += jnp.where(row == place - start, late, 0.0)
            out_ref[start : start + EDGE] = total.astype(BF16)


def patch(late_p, late_lg, fix, shorts, mixed, errors):
    vmem = pl.BlockSpec(memory_space=pltpu.VMEM)
    return pl.pallas_call(
        patch_kernel,
        in_specs=[vmem] * 8,
        out_specs=[vmem] * 4,
        out_shape=[jax.ShapeDtypeStruct(mixed.shape, BF16)] * 4,
        compiler_params=SMALL,
        name="patch",
    )(late_p, late_lg, fix, shorts, mixed, *errors)


def spread_kernel(tile_ref, short_ref, late_ref, out_ref, p_ref, lg_ref):
    peers = out_ref.shape[0]
    out_ref[:, 0:8] = jnp.broadcast_to(tile_ref[...][None], (peers, 8, 1, TILE))
    out_ref[:, 8:9] = jnp.broadcast_to(short_ref[...][None], (peers, 1, 1, TILE))
    p_ref[...] = late_ref[0:1]
    lg_ref[...] = late_ref[1:2]


def final_kernel(scale, groups, gathered_ref, filter_ref, short_ref):
    for h in range(4):
        for d in range(groups):
            for half in range(2):
                tile = gathered_ref[seat(h, d, half), 0:8].reshape(8, TILE)
                start = (d * 4 + h) * TILE
                filter_ref[8 * half : 8 * half + 8, start : start + TILE] = tile * scale
        for g in range(9):
            row = gathered_ref[seat(h, g // 2, g % 2), 8] * scale
            short_ref[g : g + 1, h * TILE : (h + 1) * TILE] = row


def on_device(q_stream, k_stream, v_stream, filter_taps, short_taps, cotangent, *, matrices):
    groups, peers = lax.axis_size("dp"), lax.axis_size("ctx")

    def shifted(value, by):
        pairs = [(i, i + by) for i in range(peers) if 0 <= i + by < peers]
        return lax.ppermute(value, "ctx", pairs)

    place = lax.axis_index("ctx").astype(jnp.int32).reshape(1)
    far, near = pack(place, q_stream, k_stream, v_stream, cotangent)
    far = lax.ppermute(
        far, "ctx", [(i, i + 1 if i % 2 else i - 1) for i in range(1, peers - 1)]
    )
    near = lax.ppermute(near, "ctx", [(i, i ^ 1) for i in range(peers)])
    taps = lax.all_to_all(filter_taps, "dp", split_axis=1, concat_axis=0, tiled=True)

    mixed, *errors, part, fix, late = run_layer(
        place,
        (q_stream, k_stream, v_stream, cotangent),
        far,
        near,
        taps,
        short_taps,
        matrices,
    )

    part = lax.all_to_all(part, "ctx", split_axis=0, concat_axis=0, tiled=True)
    vmem = pl.BlockSpec(memory_space=pltpu.VMEM)
    tile, short = pl.pallas_call(
        sum_kernel,
        in_specs=[vmem],
        out_specs=[vmem] * 2,
        out_shape=[
            jax.ShapeDtypeStruct((8, 1, TILE), F32),
            jax.ShapeDtypeStruct((1, 1, TILE), F32),
        ],
        compiler_params=SMALL,
        name="sum",
    )(part)

    pairs = [
        (d * peers + seat(h, e, half), e * peers + seat(h, d, half))
        for d in range(groups)
        for h in range(4)
        for e in range(groups)
        for half in range(2)
    ]
    tile = lax.ppermute(tile, ("dp", "ctx"), pairs)
    edge_row = jax.ShapeDtypeStruct((1, 1, q_stream.shape[1]), F32)
    sent, late_p, late_lg = pl.pallas_call(
        spread_kernel,
        out_shape=[jax.ShapeDtypeStruct((peers, CHUNK, 1, TILE), F32), edge_row, edge_row],
        compiler_params=SMALL,
        name="spread",
    )(tile, short, late)
    outs = patch(
        shifted(late_p, 1), shifted(late_lg, -1), fix, short_taps, mixed, errors
    )
    gathered = lax.all_to_all(sent, "ctx", split_axis=0, concat_axis=0, tiled=True)
    scale = 1.0 / math.sqrt(ROWS * peers)
    grad_filter, grad_short = pl.pallas_call(
        functools.partial(final_kernel, scale, groups),
        out_shape=[
            jax.ShapeDtypeStruct(filter_taps.shape, F32),
            jax.ShapeDtypeStruct(short_taps.shape, F32),
        ],
        compiler_params=SMALL,
        name="final",
    )(gathered)
    return (*outs, grad_filter, grad_short)


def solution(mesh):
    streams = P("ctx", "dp")
    in_specs = (streams, streams, streams, P("dp", None), P(None, "dp"), streams)
    out_specs = (streams,) * 4 + (P("dp", None), P(None, "dp"))
    matrices = transform_matrices()
    return jax.shard_map(
        functools.partial(on_device, matrices=matrices),
        mesh=mesh,
        in_specs=in_specs,
        out_specs=out_specs,
        check_vma=False,
    )
```

```python
import functools
import math

import jax
import jax.numpy as jnp
import ml_dtypes
import numpy as np
from jax import lax
from jax.experimental import pallas as pl
from jax.experimental.pallas import tpu as pltpu
from jax.sharding import PartitionSpec as P

BF16 = jnp.bfloat16
F32 = jnp.float32

ROWS = 128
PERIOD = 256
HALF = PERIOD // 2
OUT = 136
WIDE = 256
EDGE = 16
TILE = 128
FAR_ROWS = 288
CHUNK = 9
VMEM_LIMIT = 24 * 1024 * 1024
SMALL = pltpu.CompilerParams(vmem_limit_bytes=8 * 1024 * 1024)


def two_parts(matrix):
    high = matrix.astype(ml_dtypes.bfloat16)
    low = (matrix - high.astype(np.float64)).astype(ml_dtypes.bfloat16)
    return np.concatenate([high, low, high], 1)


def transform_matrices():
    freqs = np.arange(HALF) + 0.5

    def angles(places):
        return 2.0 * np.pi * np.outer(freqs, places) / PERIOD

    forward = angles(np.arange(PERIOD))
    forward = np.concatenate([np.cos(forward), -np.sin(forward)], 0)

    def inverse(places):
        turned = angles(places).T
        return np.concatenate([np.cos(turned), -np.sin(turned)], 1) * (2.0 / PERIOD)

    long_back = inverse(np.arange(HALF, HALF + OUT))
    grad_back = inverse(np.arange(OUT))
    return tuple(two_parts(m) for m in (forward, long_back, grad_back))


def split(value):
    high = value.astype(BF16)
    low = (value - high.astype(F32)).astype(BF16)
    return high, low


def dot3(matrix, value):
    high, low = split(value)
    parts = jnp.concatenate([high, high, low], 0)
    return jnp.dot(matrix, parts, preferred_element_type=F32)


def pack_kernel(place_ref, q_ref, k_ref, v_ref, c_ref, far_ref, near_ref):
    def to_right(ref):
        ref[0:ROWS] = k_ref[...]
        ref[ROWS : 2 * ROWS] = v_ref[...]
        ref[2 * ROWS : 2 * ROWS + EDGE] = q_ref[ROWS - EDGE : ROWS]

    def to_left(ref):
        ref[0:ROWS] = q_ref[...]
        ref[ROWS : 2 * ROWS] = c_ref[...]
        ref[2 * ROWS : 2 * ROWS + EDGE] = k_ref[0:EDGE]
        ref[2 * ROWS + EDGE : 2 * ROWS + 2 * EDGE] = v_ref[0:EDGE]

    odd = lax.rem(place_ref[0], 2) == 1

    @pl.when(odd)
    def _():
        to_right(far_ref)
        to_left(near_ref)

    @pl.when(jnp.logical_not(odd))
    def _():
        to_left(far_ref)
        to_right(near_ref)


def pack(place, q_stream, k_stream, v_stream, cotangent):
    channels = q_stream.shape[1]
    vmem = pl.BlockSpec(memory_space=pltpu.VMEM)
    return pl.pallas_call(
        pack_kernel,
        in_specs=[pl.BlockSpec(memory_space=pltpu.SMEM)] + [vmem] * 4,
        out_specs=[vmem] * 2,
        out_shape=[
            jax.ShapeDtypeStruct((FAR_ROWS, channels), BF16),
            jax.ShapeDtypeStruct((2 * ROWS + 2 * EDGE, channels), BF16),
        ],
        compiler_params=SMALL,
        name="pack",
    )(place, q_stream, k_stream, v_stream, cotangent)


def order_of(peers):
    return [(i * 29 + 7) % peers for i in range(peers)]


ORDER = order_of(64)


def seat(h, owner, half):
    return 16 * h + 8 * half + 2 * (owner % 4) + owner // 4


def layer_kernel(
    place_ref,
    q_ref, k_ref, v_ref, c_ref, far_ref, near_ref,
    h_ref, s_ref, fwd_ref, long_ref, grad_ref,
    mixed_ref, eq_ref, ek_ref, ev_ref, part_ref, fix_ref, late_ref,
    q_ext, k_ext, v_ext, c_next, short_all,
):
    def f32(x):
        return x.astype(F32)

    odd = lax.rem(place_ref[0], 2) == 1
    half = jnp.concatenate([fwd_ref[:, PERIOD * n : PERIOD * n + HALF] for n in range(3)], 1)
    freq = lax.broadcasted_iota(jnp.int32, (HALF, WIDE), 0)
    sign = jnp.where(freq % 2 == 0, 1.0, -1.0).astype(F32)
    row = lax.broadcasted_iota(jnp.int32, (8, WIDE), 0)

    def times(a, b):
        ar, ai, br, bi = a[0:HALF], a[HALF:], b[0:HALF], b[HALF:]
        return jnp.concatenate([ar * br - ai * bi, ar * bi + ai * br], 0)

    def times_conj(a, b):
        ar, ai, br, bi = a[0:HALF], a[HALF:], b[0:HALF], b[HALF:]
        return jnp.concatenate([ar * br + ai * bi, ai * br - ar * bi], 0)

    for step in range(q_ref.shape[1] // WIDE):
        cols = pl.ds(step * WIDE, WIDE)

        def stage(before_ref, after_ref):
            q_ext[0:8] = f32(before_ref[2 * ROWS : 2 * ROWS + EDGE, cols])[8:16]
            q_ext[136:264] = f32(after_ref[0:ROWS, cols])
            c_next[...] = f32(after_ref[ROWS : 2 * ROWS, cols])
            for n, ext in ((0, k_ext), (1, v_ext)):
                ext[8:136] = f32(before_ref[ROWS * n : ROWS * (n + 1), cols])
                start = 2 * ROWS + EDGE * n
                ext[264:272] = f32(after_ref[start : start + EDGE, cols])[0:8]

        @pl.when(odd)
        def _():
            stage(near_ref, far_ref)

        @pl.when(jnp.logical_not(odd))
        def _():
            stage(far_ref, near_ref)

        q_ext[8:136] = f32(q_ref[:, cols])
        for ext, own in ((k_ext, k_ref), (v_ext, v_ref)):
            ext[0:8] = jnp.zeros((8, WIDE), F32)
            ext[136:264] = f32(own[:, cols])

        def tap(s, j):
            return s_ref[3 * s + j : 3 * s + j + 1, cols]

        def causal(ext, s, count):
            return (
                tap(s, 0) * ext[8 : 8 + count]
                + tap(s, 1) * ext[7 : 7 + count]
                + tap(s, 2) * ext[6 : 6 + count]
            )

        a0 = causal(q_ext, 0, 256)
        a1 = causal(k_ext, 1, 264)
        a2 = causal(v_ext, 2, 264)
        product = a1 * a2
        p_before = jnp.concatenate([jnp.where(row < 2, 0.0, product[0:8]), product[8:128]], 0)
        p_own, p_far = product[128:256], product[256:264]
        cot = f32(c_ref[:, cols])
        cot_next = c_next[...]
        lg = jnp.concatenate([cot, cot_next], 0) * a0

        taps = h_ref[:, cols]
        own_f = dot3(half, p_own)
        before_f = dot3(half, p_before)
        moved_f = jnp.concatenate([own_f[HALF:] * sign, own_f[0:HALF] * -sign], 0)
        x_f = before_f + moved_f
        lg_f = dot3(fwd_ref[...], lg)
        h_f = dot3(half, taps)

        long = dot3(long_ref[...], times(x_f, h_f))
        pg = dot3(grad_ref[...], times_conj(lg_f, h_f))
        filt = dot3(grad_ref[0:ROWS], times_conj(lg_f, own_f))

        h0, h1, h127 = taps[0:1], taps[1:2], taps[127:128]
        p0, p1 = p_far[0:1], p_far[1:2]
        fix_long = jnp.where(row == 0, h0 * p0, jnp.where(row == 1, h0 * p1 + h1 * p0, 0.0))
        fix_grad = jnp.where(row == 1, h127 * lg[0:1], 0.0)
        long_own, long_far = long[0:128], long[128:136] + fix_long
        pg_own, pg_far = pg[0:128], pg[128:136] + fix_grad

        mixed = a0[0:128] * long_own
        mixed_ref[:, cols] = mixed.astype(BF16)

        def finish(s, err_own, err_far, ext, base, err_ref):
            err_ref[0:128, cols] = err_own
            err_ref[128:136, cols] = err_far
            for j in range(3):
                short_all[3 * s + j : 3 * s + j + 1, cols] = jnp.sum(
                    err_own * ext[base - j : base - j + 128], axis=0, keepdims=True
                )

        finish(0, cot * long_own, cot_next[0:8] * long_far, q_ext, 8, eq_ref)
        finish(1, pg_own * a2[128:256], pg_far * a2[256:264], k_ext, 136, ek_ref)
        finish(2, pg_own * a1[128:256], pg_far * a1[256:264], v_ext, 136, ev_ref)
        lacking = cot_next[0:1] * h127 * p_own[1:2]
        for j in range(3):
            short_all[j : j + 1, cols] += lacking * q_ext[136 - j : 137 - j]

        late_ref[0, :, cols] = p_own[1:2]
        late_ref[1, :, cols] = lg[128:129]
        fix_ref[0:1, cols] = mixed[0:1]
        fix_ref[1:4, cols] = jnp.zeros((3, WIDE), F32)
        fix_ref[4:5, cols] = a0[0:1] * h127
        fix_ref[5:6, cols] = tap(0, 0) * cot[0:1] * h127
        fix_ref[6:7, cols] = tap(1, 2) * h127 * a2[257:258]
        fix_ref[7:8, cols] = tap(2, 2) * h127 * a1[257:258]

        for part in range(WIDE // TILE):
            h = step * (WIDE // TILE) + part
            lanes = slice(part * TILE, (part + 1) * TILE)
            for g in range(16):
                tile = filt[8 * g : 8 * g + 8, lanes]
                part_ref[ORDER.index(seat(h, g // 2, g % 2)), 0:8] = tile.reshape(8, 1, TILE)
                if g < 9:
                    value = short_all[g : g + 1, h * TILE : (h + 1) * TILE]
                else:
                    value = jnp.zeros((1, TILE), F32)
                part_ref[ORDER.index(seat(h, g // 2, g % 2)), 8] = value


def run_layer(place, streams, far, near, taps, shorts, matrices):
    channels = streams[0].shape[1]
    out_rows = jax.ShapeDtypeStruct((ROWS, channels), BF16)
    ext = pltpu.VMEM((272, WIDE), F32)
    vmem = pl.BlockSpec(memory_space=pltpu.VMEM)
    return pl.pallas_call(
        layer_kernel,
        in_specs=[pl.BlockSpec(memory_space=pltpu.SMEM)] + [vmem] * 11,
        out_specs=[vmem] * 7,
        out_shape=[out_rows]
        + [jax.ShapeDtypeStruct((OUT, channels), F32)] * 3
        + [
            jax.ShapeDtypeStruct((64, CHUNK, 1, TILE), F32),
            jax.ShapeDtypeStruct((8, channels), F32),
            jax.ShapeDtypeStruct((2, 1, channels), F32),
        ],
        scratch_shapes=[
            ext, ext, ext,
            pltpu.VMEM((ROWS, WIDE), F32),
            pltpu.VMEM((16, channels), F32),
        ],
        compiler_params=pltpu.CompilerParams(vmem_limit_bytes=VMEM_LIMIT),
        name="layer",
    )(place, *streams, far, near, taps, shorts, *matrices)


def sum_kernel(part_ref, tile_ref, short_ref):
    total = jnp.sum(part_ref[...], axis=0)
    tile_ref[...] = total[0:8]
    short_ref[...] = total[8:9]


def patch_kernel(
    p_ref, lg_ref, fix_ref, s_ref, mixed_in, eq_ref, ek_ref, ev_ref,
    mixed_ref, gq_ref, gk_ref, gv_ref,
):
    channels = p_ref.shape[2]
    row = lax.broadcasted_iota(jnp.int32, (EDGE, channels), 0)
    mixed_ref[...] = mixed_in[...]
    value = fix_ref[0:1] + fix_ref[4:5] * p_ref[0]
    old = mixed_in[0:EDGE].astype(F32)
    mixed_ref[0:EDGE] = jnp.where(row == 0, value, old).astype(BF16)
    for s, err_ref, late_ref, place, out_ref in (
        (0, eq_ref, p_ref, 0, gq_ref),
        (1, ek_ref, lg_ref, ROWS - 1, gk_ref),
        (2, ev_ref, lg_ref, ROWS - 1, gv_ref),
    ):
        late = fix_ref[5 + s : 6 + s] * late_ref[0]
        for start in range(0, ROWS, EDGE):
            total = s_ref[3 * s : 3 * s + 1] * err_ref[start : start + EDGE]
            for j in (1, 2):
                total += s_ref[3 * s + j : 3 * s + j + 1] * err_ref[start + j : start + j + EDGE]
            if start <= place < start + EDGE:
                total += jnp.where(row == place - start, late, 0.0)
            out_ref[start : start + EDGE] = total.astype(BF16)


def patch(late_p, late_lg, fix, shorts, mixed, errors):
    vmem = pl.BlockSpec(memory_space=pltpu.VMEM)
    return pl.pallas_call(
        patch_kernel,
        in_specs=[vmem] * 8,
        out_specs=[vmem] * 4,
        out_shape=[jax.ShapeDtypeStruct(mixed.shape, BF16)] * 4,
        compiler_params=SMALL,
        name="patch",
    )(late_p, late_lg, fix, shorts, mixed, *errors)


def spread_kernel(tile_ref, short_ref, late_ref, out_ref, p_ref, lg_ref):
    peers = out_ref.shape[0]
    out_ref[:, 0:8] = jnp.broadcast_to(tile_ref[...][None], (peers, 8, 1, TILE))
    out_ref[:, 8:9] = jnp.broadcast_to(short_ref[...][None], (peers, 1, 1, TILE))
    p_ref[...] = late_ref[0:1]
    lg_ref[...] = late_ref[1:2]


def final_kernel(scale, groups, gathered_ref, filter_ref, short_ref):
    for h in range(4):
        for d in range(groups):
            for half in range(2):
                tile = gathered_ref[ORDER.index(seat(h, d, half)), 0:8].reshape(8, TILE)
                start = (d * 4 + h) * TILE
                filter_ref[8 * half : 8 * half + 8, start : start + TILE] = tile * scale
        for g in range(9):
            row = gathered_ref[ORDER.index(seat(h, g // 2, g % 2)), 8] * scale
            short_ref[g : g + 1, h * TILE : (h + 1) * TILE] = row


def on_device(q_stream, k_stream, v_stream, filter_taps, short_taps, cotangent, *, matrices):
    groups, peers = lax.axis_size("dp"), lax.axis_size("ctx")

    def shifted(value, by):
        pairs = [(i, i + by) for i in range(peers) if 0 <= i + by < peers]
        return lax.ppermute(value, "ctx", pairs)

    place = lax.axis_index("ctx").astype(jnp.int32).reshape(1)
    far, near = pack(place, q_stream, k_stream, v_stream, cotangent)
    far = lax.ppermute(
        far, "ctx", [(i, i + 1 if i % 2 else i - 1) for i in range(1, peers - 1)]
    )
    near = lax.ppermute(near, "ctx", [(i, i ^ 1) for i in range(peers)])
    taps = lax.all_to_all(filter_taps, "dp", split_axis=1, concat_axis=0, tiled=True)

    mixed, *errors, part, fix, late = run_layer(
        place,
        (q_stream, k_stream, v_stream, cotangent),
        far,
        near,
        taps,
        short_taps,
        matrices,
    )

    part = lax.all_to_all(part, "ctx", split_axis=0, concat_axis=0, tiled=True, axis_index_groups=[ORDER])
    vmem = pl.BlockSpec(memory_space=pltpu.VMEM)
    tile, short = pl.pallas_call(
        sum_kernel,
        in_specs=[vmem],
        out_specs=[vmem] * 2,
        out_shape=[
            jax.ShapeDtypeStruct((8, 1, TILE), F32),
            jax.ShapeDtypeStruct((1, 1, TILE), F32),
        ],
        compiler_params=SMALL,
        name="sum",
    )(part)

    pairs = [
        (d * peers + seat(h, e, half), e * peers + seat(h, d, half))
        for d in range(groups)
        for h in range(4)
        for e in range(groups)
        for half in range(2)
    ]
    tile = lax.ppermute(tile, ("dp", "ctx"), pairs)
    edge_row = jax.ShapeDtypeStruct((1, 1, q_stream.shape[1]), F32)
    sent, late_p, late_lg = pl.pallas_call(
        spread_kernel,
        out_shape=[jax.ShapeDtypeStruct((peers, CHUNK, 1, TILE), F32), edge_row, edge_row],
        compiler_params=SMALL,
        name="spread",
    )(tile, short, late)
    outs = patch(
        shifted(late_p, 1), shifted(late_lg, -1), fix, short_taps, mixed, errors
    )
    gathered = lax.all_to_all(sent, "ctx", split_axis=0, concat_axis=0, tiled=True, axis_index_groups=[ORDER])
    scale = 1.0 / math.sqrt(ROWS * peers)
    grad_filter, grad_short = pl.pallas_call(
        functools.partial(final_kernel, scale, groups),
        out_shape=[
            jax.ShapeDtypeStruct(filter_taps.shape, F32),
            jax.ShapeDtypeStruct(short_taps.shape, F32),
        ],
        compiler_params=SMALL,
        name="final",
    )(gathered)
    return (*outs, grad_filter, grad_short)


def solution(mesh):
    streams = P("ctx", "dp")
    in_specs = (streams, streams, streams, P("dp", None), P(None, "dp"), streams)
    out_specs = (streams,) * 4 + (P("dp", None), P(None, "dp"))
    matrices = transform_matrices()
    return jax.shard_map(
        functools.partial(on_device, matrices=matrices),
        mesh=mesh,
        in_specs=in_specs,
        out_specs=out_specs,
        check_vma=False,
    )
```

```python
import functools
import math

import jax
import jax.numpy as jnp
import ml_dtypes
import numpy as np
from jax import lax
from jax.experimental import pallas as pl
from jax.experimental.pallas import tpu as pltpu
from jax.sharding import PartitionSpec as P

BF16 = jnp.bfloat16
F32 = jnp.float32

ROWS = 128
PERIOD = 256
HALF = PERIOD // 2
OUT = 136
WIDE = 256
EDGE = 16
TILE = 128
FAR_ROWS = 288
CHUNK = 9
VMEM_LIMIT = 24 * 1024 * 1024
SMALL = pltpu.CompilerParams(vmem_limit_bytes=8 * 1024 * 1024)


def two_parts(matrix):
    high = matrix.astype(ml_dtypes.bfloat16)
    low = (matrix - high.astype(np.float64)).astype(ml_dtypes.bfloat16)
    return np.concatenate([high, low, high], 1)


def transform_matrices():
    freqs = np.arange(HALF) + 0.5

    def angles(places):
        return 2.0 * np.pi * np.outer(freqs, places) / PERIOD

    forward = angles(np.arange(PERIOD))
    forward = np.concatenate([np.cos(forward), -np.sin(forward)], 0)

    def inverse(places):
        turned = angles(places).T
        return np.concatenate([np.cos(turned), -np.sin(turned)], 1) * (2.0 / PERIOD)

    long_back = inverse(np.arange(HALF, HALF + OUT))
    grad_back = inverse(np.arange(OUT))
    return tuple(two_parts(m) for m in (forward, long_back, grad_back))


def split(value):
    high = value.astype(BF16)
    low = (value - high.astype(F32)).astype(BF16)
    return high, low


def dot3(matrix, value):
    high, low = split(value)
    parts = jnp.concatenate([high, high, low], 0)
    return jnp.dot(matrix, parts, preferred_element_type=F32)


def pack_kernel(place_ref, q_ref, k_ref, v_ref, c_ref, far_ref, near_ref):
    def to_right(ref):
        ref[0:ROWS] = k_ref[...]
        ref[ROWS : 2 * ROWS] = v_ref[...]
        ref[2 * ROWS : 2 * ROWS + EDGE] = q_ref[ROWS - EDGE : ROWS]

    def to_left(ref):
        ref[0:ROWS] = q_ref[...]
        ref[ROWS : 2 * ROWS] = c_ref[...]
        ref[2 * ROWS : 2 * ROWS + EDGE] = k_ref[0:EDGE]
        ref[2 * ROWS + EDGE : 2 * ROWS + 2 * EDGE] = v_ref[0:EDGE]

    odd = lax.rem(place_ref[0], 2) == 1

    @pl.when(odd)
    def _():
        to_right(far_ref)
        to_left(near_ref)

    @pl.when(jnp.logical_not(odd))
    def _():
        to_left(far_ref)
        to_right(near_ref)


def pack(place, q_stream, k_stream, v_stream, cotangent):
    channels = q_stream.shape[1]
    vmem = pl.BlockSpec(memory_space=pltpu.VMEM)
    return pl.pallas_call(
        pack_kernel,
        in_specs=[pl.BlockSpec(memory_space=pltpu.SMEM)] + [vmem] * 4,
        out_specs=[vmem] * 2,
        out_shape=[
            jax.ShapeDtypeStruct((FAR_ROWS, channels), BF16),
            jax.ShapeDtypeStruct((2 * ROWS + 2 * EDGE, channels), BF16),
        ],
        compiler_params=SMALL,
        name="pack",
    )(place, q_stream, k_stream, v_stream, cotangent)


def order_of(peers):
    return [(i * 35 + 7) % peers for i in range(peers)]


ORDER = order_of(64)


def seat(h, owner, half):
    return 16 * h + 8 * half + 2 * (owner % 4) + owner // 4


def layer_kernel(
    place_ref,
    q_ref, k_ref, v_ref, c_ref, far_ref, near_ref,
    h_ref, s_ref, fwd_ref, long_ref, grad_ref,
    mixed_ref, eq_ref, ek_ref, ev_ref, part_ref, fix_ref, late_ref,
    q_ext, k_ext, v_ext, c_next, short_all,
):
    def f32(x):
        return x.astype(F32)

    odd = lax.rem(place_ref[0], 2) == 1
    half = jnp.concatenate([fwd_ref[:, PERIOD * n : PERIOD * n + HALF] for n in range(3)], 1)
    freq = lax.broadcasted_iota(jnp.int32, (HALF, WIDE), 0)
    sign = jnp.where(freq % 2 == 0, 1.0, -1.0).astype(F32)
    row = lax.broadcasted_iota(jnp.int32, (8, WIDE), 0)

    def times(a, b):
        ar, ai, br, bi = a[0:HALF], a[HALF:], b[0:HALF], b[HALF:]
        return jnp.concatenate([ar * br - ai * bi, ar * bi + ai * br], 0)

    def times_conj(a, b):
        ar, ai, br, bi = a[0:HALF], a[HALF:], b[0:HALF], b[HALF:]
        return jnp.concatenate([ar * br + ai * bi, ai * br - ar * bi], 0)

    for step in range(q_ref.shape[1] // WIDE):
        cols = pl.ds(step * WIDE, WIDE)

        def stage(before_ref, after_ref):
            q_ext[0:8] = f32(before_ref[2 * ROWS : 2 * ROWS + EDGE, cols])[8:16]
            q_ext[136:264] = f32(after_ref[0:ROWS, cols])
            c_next[...] = f32(after_ref[ROWS : 2 * ROWS, cols])
            for n, ext in ((0, k_ext), (1, v_ext)):
                ext[8:136] = f32(before_ref[ROWS * n : ROWS * (n + 1), cols])
                start = 2 * ROWS + EDGE * n
                ext[264:272] = f32(after_ref[start : start + EDGE, cols])[0:8]

        @pl.when(odd)
        def _():
            stage(near_ref, far_ref)

        @pl.when(jnp.logical_not(odd))
        def _():
            stage(far_ref, near_ref)

        q_ext[8:136] = f32(q_ref[:, cols])
        for ext, own in ((k_ext, k_ref), (v_ext, v_ref)):
            ext[0:8] = jnp.zeros((8, WIDE), F32)
            ext[136:264] = f32(own[:, cols])

        def tap(s, j):
            return s_ref[3 * s + j : 3 * s + j + 1, cols]

        def causal(ext, s, count):
            return (
                tap(s, 0) * ext[8 : 8 + count]
                + tap(s, 1) * ext[7 : 7 + count]
                + tap(s, 2) * ext[6 : 6 + count]
            )

        a0 = causal(q_ext, 0, 256)
        a1 = causal(k_ext, 1, 264)
        a2 = causal(v_ext, 2, 264)
        product = a1 * a2
        p_before = jnp.concatenate([jnp.where(row < 2, 0.0, product[0:8]), product[8:128]], 0)
        p_own, p_far = product[128:256], product[256:264]
        cot = f32(c_ref[:, cols])
        cot_next = c_next[...]
        lg = jnp.concatenate([cot, cot_next], 0) * a0

        taps = h_ref[:, cols]
        own_f = dot3(half, p_own)
        before_f = dot3(half, p_before)
        moved_f = jnp.concatenate([own_f[HALF:] * sign, own_f[0:HALF] * -sign], 0)
        x_f = before_f + moved_f
        lg_f = dot3(fwd_ref[...], lg)
        h_f = dot3(half, taps)

        long = dot3(long_ref[...], times(x_f, h_f))
        pg = dot3(grad_ref[...], times_conj(lg_f, h_f))
        filt = dot3(grad_ref[0:ROWS], times_conj(lg_f, own_f))

        h0, h1, h127 = taps[0:1], taps[1:2], taps[127:128]
        p0, p1 = p_far[0:1], p_far[1:2]
        fix_long = jnp.where(row == 0, h0 * p0, jnp.where(row == 1, h0 * p1 + h1 * p0, 0.0))
        fix_grad = jnp.where(row == 1, h127 * lg[0:1], 0.0)
        long_own, long_far = long[0:128], long[128:136] + fix_long
        pg_own, pg_far = pg[0:128], pg[128:136] + fix_grad

        mixed = a0[0:128] * long_own
        mixed_ref[:, cols] = mixed.astype(BF16)

        def finish(s, err_own, err_far, ext, base, err_ref):
            err_ref[0:128, cols] = err_own
            err_ref[128:136, cols] = err_far
            for j in range(3):
                short_all[3 * s + j : 3 * s + j + 1, cols] = jnp.sum(
                    err_own * ext[base - j : base - j + 128], axis=0, keepdims=True
                )

        finish(0, cot * long_own, cot_next[0:8] * long_far, q_ext, 8, eq_ref)
        finish(1, pg_own * a2[128:256], pg_far * a2[256:264], k_ext, 136, ek_ref)
        finish(2, pg_own * a1[128:256], pg_far * a1[256:264], v_ext, 136, ev_ref)
        lacking = cot_next[0:1] * h127 * p_own[1:2]
        for j in range(3):
            short_all[j : j + 1, cols] += lacking * q_ext[136 - j : 137 - j]

        late_ref[0, :, cols] = p_own[1:2]
        late_ref[1, :, cols] = lg[128:129]
        fix_ref[0:1, cols] = mixed[0:1]
        fix_ref[1:4, cols] = jnp.zeros((3, WIDE), F32)
        fix_ref[4:5, cols] = a0[0:1] * h127
        fix_ref[5:6, cols] = tap(0, 0) * cot[0:1] * h127
        fix_ref[6:7, cols] = tap(1, 2) * h127 * a2[257:258]
        fix_ref[7:8, cols] = tap(2, 2) * h127 * a1[257:258]

        for part in range(WIDE // TILE):
            h = step * (WIDE // TILE) + part
            lanes = slice(part * TILE, (part + 1) * TILE)
            for g in range(16):
                tile = filt[8 * g : 8 * g + 8, lanes]
                part_ref[ORDER.index(seat(h, g // 2, g % 2)), 0:8] = tile.reshape(8, 1, TILE)
                if g < 9:
                    value = short_all[g : g + 1, h * TILE : (h + 1) * TILE]
                else:
                    value = jnp.zeros((1, TILE), F32)
                part_ref[ORDER.index(seat(h, g // 2, g % 2)), 8] = value


def run_layer(place, streams, far, near, taps, shorts, matrices):
    channels = streams[0].shape[1]
    out_rows = jax.ShapeDtypeStruct((ROWS, channels), BF16)
    ext = pltpu.VMEM((272, WIDE), F32)
    vmem = pl.BlockSpec(memory_space=pltpu.VMEM)
    return pl.pallas_call(
        layer_kernel,
        in_specs=[pl.BlockSpec(memory_space=pltpu.SMEM)] + [vmem] * 11,
        out_specs=[vmem] * 7,
        out_shape=[out_rows]
        + [jax.ShapeDtypeStruct((OUT, channels), F32)] * 3
        + [
            jax.ShapeDtypeStruct((64, CHUNK, 1, TILE), F32),
            jax.ShapeDtypeStruct((8, channels), F32),
            jax.ShapeDtypeStruct((2, 1, channels), F32),
        ],
        scratch_shapes=[
            ext, ext, ext,
            pltpu.VMEM((ROWS, WIDE), F32),
            pltpu.VMEM((16, channels), F32),
        ],
        compiler_params=pltpu.CompilerParams(vmem_limit_bytes=VMEM_LIMIT),
        name="layer",
    )(place, *streams, far, near, taps, shorts, *matrices)


def sum_kernel(part_ref, tile_ref, short_ref):
    total = jnp.sum(part_ref[...], axis=0)
    tile_ref[...] = total[0:8]
    short_ref[...] = total[8:9]


def patch_kernel(
    p_ref, lg_ref, fix_ref, s_ref, mixed_in, eq_ref, ek_ref, ev_ref,
    mixed_ref, gq_ref, gk_ref, gv_ref,
):
    channels = p_ref.shape[2]
    row = lax.broadcasted_iota(jnp.int32, (EDGE, channels), 0)
    mixed_ref[...] = mixed_in[...]
    value = fix_ref[0:1] + fix_ref[4:5] * p_ref[0]
    old = mixed_in[0:EDGE].astype(F32)
    mixed_ref[0:EDGE] = jnp.where(row == 0, value, old).astype(BF16)
    for s, err_ref, late_ref, place, out_ref in (
        (0, eq_ref, p_ref, 0, gq_ref),
        (1, ek_ref, lg_ref, ROWS - 1, gk_ref),
        (2, ev_ref, lg_ref, ROWS - 1, gv_ref),
    ):
        late = fix_ref[5 + s : 6 + s] * late_ref[0]
        for start in range(0, ROWS, EDGE):
            total = s_ref[3 * s : 3 * s + 1] * err_ref[start : start + EDGE]
            for j in (1, 2):
                total += s_ref[3 * s + j : 3 * s + j + 1] * err_ref[start + j : start + j + EDGE]
            if start <= place < start + EDGE:
                total += jnp.where(row == place - start, late, 0.0)
            out_ref[start : start + EDGE] = total.astype(BF16)


def patch(late_p, late_lg, fix, shorts, mixed, errors):
    vmem = pl.BlockSpec(memory_space=pltpu.VMEM)
    return pl.pallas_call(
        patch_kernel,
        in_specs=[vmem] * 8,
        out_specs=[vmem] * 4,
        out_shape=[jax.ShapeDtypeStruct(mixed.shape, BF16)] * 4,
        compiler_params=SMALL,
        name="patch",
    )(late_p, late_lg, fix, shorts, mixed, *errors)


def spread_kernel(tile_ref, short_ref, late_ref, out_ref, p_ref, lg_ref):
    peers = out_ref.shape[0]
    out_ref[:, 0:8] = jnp.broadcast_to(tile_ref[...][None], (peers, 8, 1, TILE))
    out_ref[:, 8:9] = jnp.broadcast_to(short_ref[...][None], (peers, 1, 1, TILE))
    p_ref[...] = late_ref[0:1]
    lg_ref[...] = late_ref[1:2]


def final_kernel(scale, groups, gathered_ref, filter_ref, short_ref):
    for h in range(4):
        for d in range(groups):
            for half in range(2):
                tile = gathered_ref[ORDER.index(seat(h, d, half)), 0:8].reshape(8, TILE)
                start = (d * 4 + h) * TILE
                filter_ref[8 * half : 8 * half + 8, start : start + TILE] = tile * scale
        for g in range(9):
            row = gathered_ref[ORDER.index(seat(h, g // 2, g % 2)), 8] * scale
            short_ref[g : g + 1, h * TILE : (h + 1) * TILE] = row


def on_device(q_stream, k_stream, v_stream, filter_taps, short_taps, cotangent, *, matrices):
    groups, peers = lax.axis_size("dp"), lax.axis_size("ctx")

    def shifted(value, by):
        pairs = [(i, i + by) for i in range(peers) if 0 <= i + by < peers]
        return lax.ppermute(value, "ctx", pairs)

    place = lax.axis_index("ctx").astype(jnp.int32).reshape(1)
    far, near = pack(place, q_stream, k_stream, v_stream, cotangent)
    far = lax.ppermute(
        far, "ctx", [(i, i + 1 if i % 2 else i - 1) for i in range(1, peers - 1)]
    )
    near = lax.ppermute(near, "ctx", [(i, i ^ 1) for i in range(peers)])
    taps = lax.all_to_all(filter_taps, "dp", split_axis=1, concat_axis=0, tiled=True)

    mixed, *errors, part, fix, late = run_layer(
        place,
        (q_stream, k_stream, v_stream, cotangent),
        far,
        near,
        taps,
        short_taps,
        matrices,
    )

    part = lax.all_to_all(part, "ctx", split_axis=0, concat_axis=0, tiled=True, axis_index_groups=[ORDER])
    vmem = pl.BlockSpec(memory_space=pltpu.VMEM)
    tile, short = pl.pallas_call(
        sum_kernel,
        in_specs=[vmem],
        out_specs=[vmem] * 2,
        out_shape=[
            jax.ShapeDtypeStruct((8, 1, TILE), F32),
            jax.ShapeDtypeStruct((1, 1, TILE), F32),
        ],
        compiler_params=SMALL,
        name="sum",
    )(part)

    pairs = [
        (d * peers + seat(h, e, half), e * peers + seat(h, d, half))
        for d in range(groups)
        for h in range(4)
        for e in range(groups)
        for half in range(2)
    ]
    tile = lax.ppermute(tile, ("dp", "ctx"), pairs)
    edge_row = jax.ShapeDtypeStruct((1, 1, q_stream.shape[1]), F32)
    sent, late_p, late_lg = pl.pallas_call(
        spread_kernel,
        out_shape=[jax.ShapeDtypeStruct((peers, CHUNK, 1, TILE), F32), edge_row, edge_row],
        compiler_params=SMALL,
        name="spread",
    )(tile, short, late)
    outs = patch(
        shifted(late_p, 1), shifted(late_lg, -1), fix, short_taps, mixed, errors
    )
    gathered = lax.all_to_all(sent, "ctx", split_axis=0, concat_axis=0, tiled=True, axis_index_groups=[ORDER])
    scale = 1.0 / math.sqrt(ROWS * peers)
    grad_filter, grad_short = pl.pallas_call(
        functools.partial(final_kernel, scale, groups),
        out_shape=[
            jax.ShapeDtypeStruct(filter_taps.shape, F32),
            jax.ShapeDtypeStruct(short_taps.shape, F32),
        ],
        compiler_params=SMALL,
        name="final",
    )(gathered)
    return (*outs, grad_filter, grad_short)


def solution(mesh):
    streams = P("ctx", "dp")
    in_specs = (streams, streams, streams, P("dp", None), P(None, "dp"), streams)
    out_specs = (streams,) * 4 + (P("dp", None), P(None, "dp"))
    matrices = transform_matrices()
    return jax.shard_map(
        functools.partial(on_device, matrices=matrices),
        mesh=mesh,
        in_specs=in_specs,
        out_specs=out_specs,
        check_vma=False,
    )
```
